128 devices in a mesh: ty: 16 (over x, y), tx: 8 (over z, core).
Axes of the slice: x: 4, y: 4, z: 4, core: 2. Of those that a mesh axis runs over, the one named last changes fastest.
Arguments:
- specimen: float32 [2, 8192, 2048], P(None, 'ty', 'tx'), may hold values from -5 to 5
- probe_wave: float32 [2, 256, 256], replicated, may hold values from -6 to 6
- amplitudes: bfloat16 [128, 24, 256, 256], P(('ty', 'tx')), may hold values from 0.19921875 to 2.5
- counts: int32 [128], P(('ty', 'tx')), may hold values from 1 to 24, 1024 in all
- offsets: int32 [128, 24, 2], P(('ty', 'tx')), may hold values from 0 to 7936, as said below
Outputs:
- refined: float32 [2, 8192, 2048], P(None, 'ty', 'tx')
- misfits: float32 [2], replicated
The draws below stay inside these ranges and needn't reach their ends.
Inputs may be any that keep to these rules, and one draw needn't show every extreme that they name: Slots s < counts[d] of device d hold its patterns, the other slots hold none; the counts add up to 1024, and some device holds exactly 24. offsets[d, s] lies in device d's own tile of 512 x 256 object pixels, and the whole 256 x 256 patch lies inside the object.
All inputs are finite; a program needn't handle non-finite values.
Results may differ from the reference program's by a relative error of at most 0.0027.
Values may be sent and summed in bfloat16 or wider, within the bound.
A program may use at most 128 MiB of HBM per device.

```python
import math
import jax
import jax.numpy as jnp
import numpy as np
from jax import lax

PIXELS = 256
TILE_R = 512
TILE_C = 256
MEAN_DEV = 8
ROUNDS = 2
BUNDLE = 4
SLOTS = 24
PATTERNS = 1024
OBJ_ROWS = 8192
OBJ_COLS = 2048
N_TY = 16
N_TX = 8


def draw_offsets(key, part):
    key = jax.random.fold_in(key, 7)
    devices_all = N_TY * N_TX
    device_ids = jnp.arange(devices_all, dtype=jnp.int32)
    tile_row = device_ids // N_TX
    tile_col = device_ids % N_TX
    row_high = jnp.where(tile_row == N_TY - 1, TILE_R - PIXELS + 1, TILE_R)
    col_high = jnp.where(tile_col == N_TX - 1, TILE_C - PIXELS + 1, TILE_C)
    first_key, second_key = jax.random.split(key)
    rows = jax.random.randint(first_key, (devices_all, SLOTS), 0, row_high[:, None]) + tile_row[:, None] * TILE_R
    cols = jax.random.randint(second_key, (devices_all, SLOTS), 0, col_high[:, None]) + tile_col[:, None] * TILE_C
    rows = rows.at[0, 0].set(0).at[devices_all - 1, 0].set(N_TY * TILE_R - PIXELS)
    cols = cols.at[0, 0].set(0).at[devices_all - 1, 0].set(N_TX * TILE_C - PIXELS)
    return jnp.stack([rows, cols], axis=-1).astype(jnp.int32)


def level_of(stream_key, extent, cuts, smallest, high):
    factor_of, own = 1.0, jax.random.fold_in(stream_key, 6)
    for position, shards_of in cuts:
        heights = jnp.exp(jax.random.uniform(jax.random.fold_in(own, position), (shards_of,), jnp.float32, smallest / len(cuts), high / len(cuts)))
        factor_of = factor_of * jnp.repeat(heights, extent[position] // shards_of).reshape([-1 if axis == position else 1 for axis in range(len(extent))])
    return factor_of


def profile(amount, total, limit, skew):
    portions = [(1 << 20) // math.isqrt(grade ** skew) + 1 for grade in range(2, amount + 1)]
    spare, given = total - limit - (amount - 1), [1] * (amount - 1)
    while spare > 0:
        movable = [i for i in range(amount - 1) if given[i] < limit]
        pool, budget = sum([portions[i] for i in movable]), spare
        for i in movable:
            more = min(limit - given[i], max(1, budget * portions[i] // pool), spare)
            given[i] = given[i] + more
            spare = spare - more
    return np.array([limit] + given)


def uneven_parts(own_key, amount, total, most, lean):
    if amount == 2:
        one = jax.random.randint(own_key, (), max(1, total - most), min(most, total - 1) + 1)
        return jnp.stack([one, total - one])
    lengths = jnp.asarray(profile(amount, total, most, lean), jnp.int32)
    couples = (amount - 1) // 2
    giver, taker = lengths[1:1 + 2 * couples:2], lengths[2:2 + 2 * couples:2]
    margin = jnp.minimum(giver - 1, most - taker)
    shifted = jax.random.randint(jax.random.fold_in(own_key, 1), (couples,), 0, 1 << 20) % (margin + 1)
    lengths = lengths.at[1:1 + 2 * couples:2].set(giver - shifted).at[2:2 + 2 * couples:2].set(taker + shifted)
    return lengths[jax.random.permutation(jax.random.fold_in(own_key, 2), amount)]


def scatter_about(rng, dims, width, reach, shards=(), kind=jnp.bfloat16):
    gain = level_of(rng, dims, shards, -0.22, 0.18) if shards else 1.0
    values = jax.random.normal(rng, dims, jnp.float32) * width * gain
    return jnp.minimum(jnp.maximum(values, -reach), reach).astype(kind)


def setup_inputs(seed: int = 0) -> dict:
    keys = jax.random.split(jax.random.key(seed), 6)
    specimen = scatter_about(keys[0], (2, OBJ_ROWS, OBJ_COLS), 0.7, 5.0, ((1, 16), (2, 8)), jnp.float32)
    probe_wave = scatter_about(keys[1], (2, PIXELS, PIXELS), 1.0, 6.0, (), jnp.float32)
    amplitudes = jnp.clip(0.19921875 + 2.3007812 * jax.random.uniform(keys[2], (N_TY * N_TX, SLOTS, PIXELS, PIXELS), jnp.float32) ** level_of(keys[2], (N_TY * N_TX, SLOTS, PIXELS, PIXELS), ((0, 128),), -0.2, 0.2), 0.19921875, 2.5).astype(jnp.bfloat16)
    counts = uneven_parts(keys[3], N_TY * N_TX, MEAN_DEV * N_TY * N_TX, SLOTS, 2).astype(jnp.int32)
    offsets = draw_offsets(jax.random.fold_in(keys[5], 71), 0)
    return dict(specimen=specimen, probe_wave=probe_wave, amplitudes=amplitudes, counts=counts, offsets=offsets)


rate_step = 0.1
floor_level = 0.5
epsilon_sq = 1e-06

def fourier_tables(size, sign):
    steps_idx = jnp.arange(size, dtype=jnp.int32)
    product = steps_idx[:, None] * steps_idx[None, :] % size
    angle = product.astype(jnp.float32) * (2.0 * math.pi / size)
    real_part = jnp.cos(angle) / math.sqrt(size)
    imag_part = -sign * jnp.sin(angle) / math.sqrt(size)
    left_side = jnp.stack([jnp.stack([real_part, -imag_part]), jnp.stack([imag_part, real_part])])
    right_side = jnp.stack([jnp.stack([real_part, imag_part]), jnp.stack([-imag_part, real_part])])
    return (left_side.astype(jnp.bfloat16), right_side.astype(jnp.bfloat16))

def complex_times(probe_wave, patches):
    real_part = probe_wave[0] * patches[:, 0] - probe_wave[1] * patches[:, 1]
    imag_part = probe_wave[0] * patches[:, 1] + probe_wave[1] * patches[:, 0]
    return jnp.stack([real_part, imag_part], axis=1)

def modulus_gradient(waves, targets, probe_wave, tables):
    left_f, right_f, left_b, right_b = tables
    near = jnp.einsum('dcuk,bckx->bdux', left_f.astype(jnp.float32), waves.astype(jnp.float32)).astype(jnp.bfloat16)
    spectrum = jnp.einsum('bcux,cdxv->bduv', near.astype(jnp.float32), right_f.astype(jnp.float32))
    modulus = jnp.sqrt(spectrum[:, 0] * spectrum[:, 0] + spectrum[:, 1] * spectrum[:, 1])
    target = targets.astype(jnp.float32)
    terms = lax.optimization_barrier(jnp.sum((modulus - target) ** 2, axis=(1, 2)))
    factor = 1.0 - target / jnp.maximum(modulus, floor_level)
    residual_wave = (spectrum * factor[:, None]).astype(jnp.bfloat16)
    back_near = jnp.einsum('dcuk,bckx->bdux', left_b.astype(jnp.float32), residual_wave.astype(jnp.float32)).astype(jnp.bfloat16)
    back = jnp.einsum('bcux,cdxv->bduv', back_near.astype(jnp.float32), right_b.astype(jnp.float32))
    grad_real = probe_wave[0] * back[:, 0] + probe_wave[1] * back[:, 1]
    grad_imag = probe_wave[0] * back[:, 1] - probe_wave[1] * back[:, 0]
    return (jnp.stack([grad_real, grad_imag], axis=1), terms)

def reference(specimen, probe_wave, amplitudes, counts, offsets):
    left_f, right_f = fourier_tables(PIXELS, 1.0)
    left_b, right_b = fourier_tables(PIXELS, -1.0)
    tables = (left_f, right_f, left_b, right_b)
    zero_index = jnp.zeros((), jnp.int32)
    slot_ids = jnp.arange(SLOTS, dtype=jnp.int32)
    live = (slot_ids[None, :] < counts[:, None]).reshape(-1)
    order = jnp.nonzero(live, size=PATTERNS)[0].astype(jnp.int32)
    flat_offsets = jnp.take(offsets.reshape(-1, 2), order, axis=0).astype(jnp.int32)
    flat_amps = amplitudes.reshape(-1, PIXELS, PIXELS)
    misfit_list = []
    current = specimen
    for round_index in range(ROUNDS):

        def block_step(block_index, running):
            gradient, misfit = running
            picks = jnp.asarray(block_index).astype(jnp.int32) * BUNDLE + jnp.arange(BUNDLE, dtype=jnp.int32)
            corners = jnp.take(flat_offsets, picks, axis=0).astype(jnp.int32)
            targets = jnp.take(flat_amps, jnp.take(order, picks), axis=0)
            patches = jax.vmap(lambda corner: lax.dynamic_slice(current, (zero_index, corner[0], corner[1]), (2, PIXELS, PIXELS)))(corners)
            waves = complex_times(probe_wave, patches).astype(jnp.bfloat16)
            grads, terms = modulus_gradient(waves, targets, probe_wave, tables)
            for member in range(BUNDLE):
                corner = corners[member]
                start = (zero_index, corner[0], corner[1])
                placed = lax.dynamic_slice(gradient, start, (2, PIXELS, PIXELS))
                gradient = lax.dynamic_update_slice(gradient, placed + grads[member], start)
            return (gradient, misfit + jnp.sum(terms))
        gradient, misfit = lax.fori_loop(0, PATTERNS // BUNDLE, block_step, (jnp.zeros_like(current), jnp.zeros((), jnp.float32)))
        scale = jnp.sqrt(jnp.sum(gradient * gradient) / (OBJ_ROWS * OBJ_COLS) + epsilon_sq)
        current = current - rate_step * gradient / scale
        misfit_list.append(misfit / (PATTERNS * PIXELS * PIXELS))
    return (current, jnp.stack(misfit_list))
```

```python
import functools

import jax
import jax.numpy as jnp
import ml_dtypes
import numpy as np
from jax import lax
from jax.experimental import pallas as pl
from jax.experimental.pallas import tpu as pltpu
from jax.sharding import PartitionSpec as P

MESH = pl.DeviceIdType.MESH
f32, bf16 = jnp.float32, jnp.bfloat16
NY, NX = 16, 8
EXT = (2, 2, 2, 2, 384, 128)
AREA = 8192.0 * 2048.0
RATE = 0.1
EPS = 1e-6
FLOOR_INV = 2.0
MIS_TOTAL = 1024.0 * 65536.0


def tables():
    n = 256
    k = np.arange(n)
    ang = (k[:, None] * k[None, :] % n) * (2 * np.pi / n)
    fr, fi = np.cos(ang) / 16.0, -np.sin(ang) / 16.0
    out = []
    for p in range(2):
        r, i = fr[:128, p::2], fi[:128, p::2]
        out.append(np.block([[r, -i], [i, r]]))
    for p in range(2):
        out.append(out[p].T)
    return np.stack(out).astype(ml_dtypes.bfloat16)


def split_columns():
    m = np.zeros((256, 256), np.float32)
    k = np.arange(256)
    m[k, (k % 2) * 128 + k // 2] = 1.0
    return m.astype(ml_dtypes.bfloat16)


def dot(a, b):
    return jnp.dot(a, b, preferred_element_type=f32)


def remote(src, dst, sems, rems, i, dev):
    return pltpu.make_async_remote_copy(
        src_ref=src, dst_ref=dst, send_sem=sems.at[i], recv_sem=rems.at[i], device_id=dev, device_id_type=MESH
    )


def places():
    ty, tx = lax.axis_index("ty"), lax.axis_index("tx")
    left, right = (ty, lax.rem(tx + NX - 1, NX)), (ty, lax.rem(tx + 1, NX))
    above, below = (lax.rem(ty + NY - 1, NY), tx), (lax.rem(ty + 1, NY), tx)
    return ty, tx, left, right, above, below


def halo_kernel(spec_ref, perm_ref, ext_ref, tmp, ss, rs):
    ty, tx, left, right, above, below = places()
    bar = pltpu.get_barrier_semaphore()
    for dev in (right, below):
        pl.semaphore_signal(bar, inc=1, device_id=dev, device_id_type=MESH)
    perm = perm_ref[...]
    for pln in range(2):
        w = dot(spec_ref[pln].astype(bf16), perm)
        tmp[pln, 0] = w[:, :128]
        tmp[pln, 1] = w[:, 128:]
    for pln in range(2):
        for rp in range(2):
            for cp in range(2):
                ext_ref[pln, rp, cp, 0, 0:256, :] = tmp[pln, cp, pl.ds(rp, 256, stride=2), :].astype(bf16)
    pl.semaphore_wait(bar, 2)
    top, own, low = slice(0, 128), slice(0, 256), slice(256, 384)

    def block(pln, ct, rows):
        return ext_ref.at[pln, :, :, ct, rows, :]

    a = remote(block(0, 0, top), block(0, 0, low), ss, rs, 0, above)
    c = remote(block(1, 0, top), block(1, 1, top), ss, rs, 1, left)
    b = remote(block(1, 0, top), block(1, 0, low), ss, rs, 2, above)
    d = remote(block(0, 0, own), block(0, 1, own), ss, rs, 3, left)
    e = remote(block(1, 0, slice(128, 256)), block(1, 1, slice(128, 256)), ss, rs, 4, left)
    corner0 = remote(block(0, 0, low), block(0, 1, low), ss, rs, 5, left)
    corner1_up = remote(block(1, 1, top), block(1, 1, low), ss, rs, 6, above)
    corner1_left = remote(block(1, 0, low), block(1, 1, low), ss, rs, 6, left)
    odd = lax.rem(tx, 2) == 1
    for copy in (a, c, b, d, e):
        copy.start()
    c.wait_recv()

    @pl.when(odd)
    def _():
        corner1_up.start()

    a.wait_recv()
    corner0.start()
    b.wait_recv()

    @pl.when(odd)
    def _():
        corner1_left.start()

    d.wait_recv()
    e.wait_recv()
    corner0.wait_recv()
    corner1_up.wait_recv()
    for copy in (a, c, b, d, e, corner0):
        copy.wait_send()

    @pl.when(odd)
    def _():
        corner1_up.wait_send()
        corner1_left.wait_send()


def pattern_kernel(first, n_ref, off_ref, ext_ref, *refs):
    if first:
        probe_ref, tab_ref, amp_ref, g_ref, mis_ref, obj, prol = refs
        obj[...] = ext_ref[...].astype(f32)
    else:
        tot_ref, alpha_ref, probe_ref, tab_ref, amp_ref, g_ref, mis_ref, obj, prol = refs
        obj[...] = ext_ref[...].astype(f32) - alpha_ref[0:1, :] * tot_ref[...]
    g_ref[...] = jnp.zeros_like(g_ref)
    mis_ref[...] = jnp.zeros_like(mis_ref)
    lane = lax.broadcasted_iota(jnp.int32, (128, 128), 1)

    def one(s, _):
        r = off_ref[s, 0]
        c = off_ref[s, 1]
        rho = r & 1
        sig = c & 1
        st = (r >> 1, (r + rho) >> 1)
        par = (rho, 1 - rho)
        masks = [lane * 2 + cp >= c for cp in range(2)]
        for cp in range(2):
            pp = cp ^ sig
            sh = (c + pp - cp) >> 1
            for q in range(2):
                for pln in range(2):
                    prol[pln, q, cp] = pltpu.roll(probe_ref[pln, q, pp], sh & 127, 1)
        T = []
        for q in range(2):
            halves = []
            sl = pl.ds(st[q], 128)
            for cp in range(2):
                o = [
                    jnp.where(masks[cp], obj[pln, par[q], cp, 0, sl, :], obj[pln, par[q], cp, 1, sl, :])
                    for pln in range(2)
                ]
                pr, pi = prol[0, q, cp], prol[1, q, cp]
                wr = pr * o[0] - pi * o[1]
                wi = pr * o[1] + pi * o[0]
                halves.append(jnp.concatenate([wr.astype(bf16), wi.astype(bf16)], axis=0))
            T.append(dot(tab_ref[q], jnp.concatenate(halves, axis=1)))
        lo = (T[0] + T[1]).astype(bf16)
        hi = (T[0] - T[1]).astype(bf16)
        X = []
        for cp in range(2):
            cs = slice(cp * 128, cp * 128 + 128)
            lhs = jnp.concatenate(
                [
                    jnp.concatenate([lo[:128, cs], lo[128:, cs]], axis=1),
                    jnp.concatenate([hi[:128, cs], hi[128:, cs]], axis=1),
                ],
                axis=0,
            )
            X.append(dot(lhs, tab_ref[2 + cp]))
        res = []
        mis = jnp.zeros((8, 128), f32)
        for h in range(2):
            S = X[0] + X[1] if h == 0 else X[0] - X[1]
            sr, si = S[:, :128], S[:, 128:]
            a = amp_ref[s, :, h * 128 : h * 128 + 128].astype(f32)
            m2 = jnp.maximum(sr * sr + si * si, 1e-30)
            rs = lax.rsqrt(m2)
            dm = m2 * rs - a
            mis = mis + jnp.sum((dm * dm).reshape(32, 8, 128), axis=0)
            f = 1.0 - a * jnp.minimum(rs, FLOOR_INV)
            res.append(S * jnp.concatenate([f, f], axis=1))
        mis_ref[...] += mis
        Y = []
        for cp in range(2):
            b = (res[0] + res[1] if cp == 0 else res[0] - res[1]).astype(bf16)
            Y.append(dot(b, tab_ref[cp]))
        for q in range(2):
            cols = []
            for cp in range(2):
                y = Y[cp][:128] + Y[cp][128:] if q == 0 else Y[cp][:128] - Y[cp][128:]
                y = y.astype(bf16)
                cols.append(jnp.concatenate([y[:, :128], y[:, 128:]], axis=0))
            z = dot(tab_ref[2 + q], jnp.concatenate(cols, axis=1))
            sl = pl.ds(st[q], 128)
            for cp in range(2):
                pr, pi = prol[0, q, cp], prol[1, q, cp]
                zr, zi = z[:128, cp * 128 : cp * 128 + 128], z[128:, cp * 128 : cp * 128 + 128]
                gg = (pr * zr + pi * zi, pr * zi - pi * zr)
                for pln in range(2):
                    g0 = jnp.where(masks[cp], gg[pln], 0.0)
                    g_ref[pln, par[q], cp, 0, sl, :] += g0
                    g_ref[pln, par[q], cp, 1, sl, :] += gg[pln] - g0
        return 0

    lax.fori_loop(0, n_ref[0], one, 0)


def group_barrier(ty, tx):
    bar = pltpu.get_barrier_semaphore()
    for k in range(1, NY):
        pl.semaphore_signal(bar, inc=1, device_id=(lax.rem(ty + k, NY), tx), device_id_type=MESH)
    for k in range(1, NX):
        pl.semaphore_signal(bar, inc=1, device_id=(ty, lax.rem(tx + k, NX)), device_id_type=MESH)
    return bar


def sum_vector(sq, mis):
    row = lax.broadcasted_iota(jnp.int32, (8, 128), 0)
    sq = jnp.sum(sq, axis=0, keepdims=True)
    mis = jnp.sum(mis, axis=0, keepdims=True)
    return jnp.where(row == 0, sq, jnp.where(row == 1, mis, 0.0))


def all_sum(vec, ty, tx, ybuf, xbuf, ys, yr, xs, xr, beside=None):
    ybuf[ty] = vec
    for k in range(1, NY):
        remote_to(ybuf.at[ty], ybuf.at[ty], ys.at[k], yr.at[ty], (lax.rem(ty + k, NY), tx)).start()
    if beside is not None:
        beside()
    for k in range(1, NY):
        j = lax.rem(ty + k, NY)
        remote_to(ybuf.at[j], ybuf.at[j], ys.at[k], yr.at[j], (j, tx)).wait_recv()
    total = ybuf[0]
    for j in range(1, NY):
        total = total + ybuf[j]
    xbuf[tx] = total
    for k in range(1, NX):
        remote_to(xbuf.at[tx], xbuf.at[tx], xs.at[k], xr.at[tx], (ty, lax.rem(tx + k, NX))).start()
    for k in range(1, NX):
        j = lax.rem(tx + k, NX)
        remote_to(xbuf.at[j], xbuf.at[j], xs.at[k], xr.at[j], (ty, j)).wait_recv()
    total = xbuf[0]
    for j in range(1, NX):
        total = total + xbuf[j]
    for k in range(1, NY):
        remote_to(ybuf.at[ty], ybuf.at[ty], ys.at[k], yr.at[ty], (lax.rem(ty + k, NY), tx)).wait_send()
    for k in range(1, NX):
        remote_to(xbuf.at[tx], xbuf.at[tx], xs.at[k], xr.at[tx], (ty, lax.rem(tx + k, NX))).wait_send()
    return total


def remote_to(src, dst, ssem, rsem, dev):
    return pltpu.make_async_remote_copy(
        src_ref=src, dst_ref=dst, send_sem=ssem, recv_sem=rsem, device_id=dev, device_id_type=MESH
    )


def step_size(total):
    sq = jnp.sum(total[0:1, :], axis=1, keepdims=True) / AREA + EPS
    return RATE * lax.rsqrt(jnp.broadcast_to(sq, (8, 128)))


SUM_SCRATCH = [
    pltpu.VMEM((NY, 8, 128), f32),
    pltpu.VMEM((NX, 8, 128), f32),
    pltpu.SemaphoreType.DMA((NY,)),
    pltpu.SemaphoreType.DMA((NY,)),
    pltpu.SemaphoreType.DMA((NX,)),
    pltpu.SemaphoreType.DMA((NX,)),
]


def spread_kernel(g_ref, mis_ref, tot_ref, sum_ref, alpha_ref, zsend, ysend, zrecv, yrecv, ss, rs, *sums):
    ty, tx, left, right, above, below = places()
    bar = group_barrier(ty, tx)
    ends = (slice(0, 128), slice(256, 384))
    for ct in range(2):
        zsend[0, ct] = g_ref[0, :, :, ct].astype(bf16)
    for e in range(2):
        ysend[1, e] = g_ref[1, :, :, :, ends[e], :].astype(bf16)
    pl.semaphore_wait(bar, NY + NX - 2)
    z = [[remote(zsend.at[p, ct], zrecv.at[p, 1 - ct], ss, rs, 4 * p + ct, (left, right)[ct]) for ct in range(2)] for p in range(2)]
    y = [[remote(ysend.at[p, e], yrecv.at[p, 1 - e], ss, rs, 4 * p + 2 + e, (above, below)[e]) for e in range(2)] for p in range(2)]
    for copy in z[0] + y[1]:
        copy.start()
    tot_ref[...] = g_ref[...]
    for ct in range(2):
        z[0][1 - ct].wait_recv()
        tot_ref[0, :, :, ct] += zrecv[0, ct].astype(f32)
    for e in range(2):
        ysend[0, e] = tot_ref[0, :, :, :, ends[e], :].astype(bf16)
        y[0][e].start()
    for e in range(2):
        y[1][1 - e].wait_recv()
        tot_ref[1, :, :, :, ends[e], :] += yrecv[1, e].astype(f32)
    for ct in range(2):
        zsend[1, ct] = tot_ref[1, :, :, ct].astype(bf16)
        z[1][ct].start()
    for e in range(2):
        y[0][1 - e].wait_recv()
        tot_ref[0, :, :, :, ends[e], :] += yrecv[0, e].astype(f32)
    for ct in range(2):
        z[1][1 - ct].wait_recv()
        tot_ref[1, :, :, ct] += zrecv[1, ct].astype(f32)
    own = tot_ref[:, :, :, 0, 0:256, :]
    sq = jnp.sum((own * own).reshape(256, 8, 128), axis=0)
    total = all_sum(sum_vector(sq, mis_ref[...]), ty, tx, *sums)
    sum_ref[...] = total
    alpha_ref[...] = step_size(total)
    for copy in z[0] + z[1] + y[0] + y[1]:
        copy.wait_send()


def final_kernel(
    g_ref, mis_ref, tot_ref, sum_ref, alpha_ref, spec_ref, perm_ref, out_ref, misfit_ref, zsend, ysend, zrecv, yrecv, own, before, mixed, ss, rs, *sums
):
    ty, tx, left, right, above, below = places()
    bar = group_barrier(ty, tx)
    low = slice(256, 384)
    zsend[0] = g_ref[0, :, :, 1].astype(bf16)
    ysend[1] = g_ref[1, :, :, :, low, :].astype(bf16)
    pl.semaphore_wait(bar, NY + NX - 2)
    z0 = remote(zsend.at[0], zrecv.at[0], ss, rs, 0, right)
    y1 = remote(ysend.at[1], yrecv.at[1], ss, rs, 1, below)
    y0 = remote(ysend.at[0, :, :, 0], yrecv.at[0, :, :, 0], ss, rs, 2, below)
    z1 = remote(zsend.at[1, :, :, 0:256], zrecv.at[1, :, :, 0:256], ss, rs, 3, right)
    z0.start()
    y1.start()
    y1.wait_recv()
    t1 = g_ref[1, :, :, 1, 0:256, :]
    zsend[1, :, :, 0:128, :] = (t1[:, :, 0:128] + yrecv[1, :, :, 1].astype(f32)).astype(bf16)
    zsend[1, :, :, 128:256, :] = t1[:, :, 128:].astype(bf16)
    z1.start()
    z0.wait_recv()
    ysend[0, :, :, 0] = (g_ref[0, :, :, 0, low, :] + zrecv[0, :, :, low, :].astype(f32)).astype(bf16)
    y0.start()
    own[0] = g_ref[0, :, :, 0, 0:256, :] + zrecv[0, :, :, 0:256, :].astype(f32)
    own[1] = g_ref[1, :, :, 0, 0:256, :]
    own[1, :, :, 0:128, :] += yrecv[1, :, :, 0].astype(f32)
    z1.wait_recv()
    own[1] += zrecv[1, :, :, 0:256, :].astype(f32)
    y0.wait_recv()
    own[0, :, :, 0:128, :] += yrecv[0, :, :, 0].astype(f32)
    mine = own[...]
    sq = jnp.sum((mine * mine).reshape(256, 8, 128), axis=0)

    def interleave(pln, rp, value):
        hi = value.astype(bf16)
        lo = (value - hi.astype(f32)).astype(bf16)
        perm = perm_ref[...]
        return dot(hi, perm) + dot(lo, perm)

    def beside():
        alpha = alpha_ref[0:1, :]
        for pln in range(2):
            for rp in range(2):
                first = alpha * tot_ref[pln, rp, :, 0, 0:256, :]
                w = interleave(pln, rp, jnp.concatenate([first[0], first[1]], axis=1))
                for h in range(2):
                    before[pln, h, pl.ds(rp, 256, stride=2), :] = w[:, h * 128 : h * 128 + 128]
                second = own[pln, rp]
                w = interleave(pln, rp, jnp.concatenate([second[0], second[1]], axis=1))
                for h in range(2):
                    mixed[pln, h, pl.ds(rp, 256, stride=2), :] = w[:, h * 128 : h * 128 + 128]

    total = all_sum(sum_vector(sq, mis_ref[...]), ty, tx, *sums, beside=beside)
    alpha = step_size(total)[0:1, :]
    for pln in range(2):
        for h in range(2):
            cols = slice(h * 128, h * 128 + 128)
            out_ref[pln, :, cols] = spec_ref[pln, :, cols] - before[pln, h] - alpha * mixed[pln, h]
    misfit_ref[0] = jnp.sum(sum_ref[1:2, :]) / MIS_TOTAL
    misfit_ref[1] = jnp.sum(total[1:2, :]) / MIS_TOTAL
    for copy in (z0, y1, y0, z1):
        copy.wait_send()


VM = pl.BlockSpec(memory_space=pltpu.VMEM)
SM = pl.BlockSpec(memory_space=pltpu.SMEM)


def params(cid=None):
    if cid is None:
        return pltpu.CompilerParams(vmem_limit_bytes=48 << 20)
    return pltpu.CompilerParams(vmem_limit_bytes=48 << 20, collective_id=cid, has_side_effects=True)


def shape(dims, t):
    return jax.ShapeDtypeStruct(dims, t)


def patterns(first, *args):
    return pl.pallas_call(
        functools.partial(pattern_kernel, first),
        out_shape=(shape(EXT, f32), shape((8, 128), f32)),
        in_specs=[SM, SM] + [VM] * (len(args) - 2),
        out_specs=(VM, VM),
        scratch_shapes=[pltpu.VMEM(EXT, f32), pltpu.VMEM((2, 2, 2, 128, 128), f32)],
        compiler_params=params(),
        name="patterns",
    )(*args)


def body(specimen, probe_wave, amplitudes, counts, offsets):
    ty, tx = lax.axis_index("ty"), lax.axis_index("tx")
    off = offsets[0] - jnp.stack([ty * 512, tx * 256])[None, :]
    probe = probe_wave.reshape(2, 128, 2, 128, 2).transpose(0, 2, 4, 1, 3)
    amp = amplitudes[0]
    tab = jnp.asarray(tables())
    split = jnp.asarray(split_columns())
    ext = pl.pallas_call(
        halo_kernel,
        out_shape=shape(EXT, bf16),
        in_specs=[VM, VM],
        out_specs=VM,
        scratch_shapes=[pltpu.VMEM((2, 2, 512, 128), f32), pltpu.SemaphoreType.DMA((7,)), pltpu.SemaphoreType.DMA((7,))],
        compiler_params=params(0),
        name="halo",
    )(specimen, split)
    g1, mis1 = patterns(True, counts, off, ext, probe, tab, amp)
    tot1, sum1, alpha1 = pl.pallas_call(
        spread_kernel,
        out_shape=(shape(EXT, f32), shape((8, 128), f32), shape((8, 128), f32)),
        in_specs=[VM] * 2,
        out_specs=(VM,) * 3,
        scratch_shapes=[
            pltpu.VMEM((2, 2, 2, 2, 384, 128), bf16),
            pltpu.VMEM((2, 2, 2, 2, 2, 128, 128), bf16),
            pltpu.VMEM((2, 2, 2, 2, 384, 128), bf16),
            pltpu.VMEM((2, 2, 2, 2, 2, 128, 128), bf16),
            pltpu.SemaphoreType.DMA((8,)),
            pltpu.SemaphoreType.DMA((8,)),
            *SUM_SCRATCH,
        ],
        compiler_params=params(1),
        name="spread",
    )(g1, mis1)
    g2, mis2 = patterns(False, counts, off, ext, tot1, alpha1, probe, tab, amp)
    refined, misfits = pl.pallas_call(
        final_kernel,
        out_shape=(shape((2, 512, 256), f32), shape((2,), f32)),
        in_specs=[VM] * 7,
        out_specs=(VM, SM),
        scratch_shapes=[
            pltpu.VMEM((2, 2, 2, 384, 128), bf16),
            pltpu.VMEM((2, 2, 2, 2, 128, 128), bf16),
            pltpu.VMEM((2, 2, 2, 384, 128), bf16),
            pltpu.VMEM((2, 2, 2, 2, 128, 128), bf16),
            pltpu.VMEM((2, 2, 2, 256, 128), f32),
            pltpu.VMEM((2, 2, 512, 128), f32),
            pltpu.VMEM((2, 2, 512, 128), f32),
            pltpu.SemaphoreType.DMA((4,)),
            pltpu.SemaphoreType.DMA((4,)),
            *SUM_SCRATCH,
        ],
        compiler_params=params(2),
        name="final",
    )(g2, mis2, tot1, sum1, alpha1, specimen, jnp.asarray(split_columns().T))
    return refined, misfits


def solution(mesh):
    return jax.shard_map(
        body,
        mesh=mesh,
        in_specs=(P(None, "ty", "tx"), P(), P(("ty", "tx"), None, None, None), P(("ty", "tx")), P(("ty", "tx"), None, None)),
        out_specs=(P(None, "ty", "tx"), P()),
        check_vma=False,
    )
```

```python
import functools

import jax
import jax.numpy as jnp
import ml_dtypes
import numpy as np
from jax import lax
from jax.experimental import pallas as pl
from jax.experimental.pallas import tpu as pltpu
from jax.sharding import PartitionSpec as P

MESH = pl.DeviceIdType.MESH
f32, bf16 = jnp.float32, jnp.bfloat16
NY, NX = 16, 8
U = 4
EXT = (2, 2, 2, 2, 384, 128)
AREA = 8192.0 * 2048.0
RATE = 0.1
EPS = 1e-6
FLOOR_INV = 2.0
MIS_TOTAL = 1024.0 * 65536.0


def tables():
    n = 256
    k = np.arange(n)
    ang = (k[:, None] * k[None, :] % n) * (2 * np.pi / n)
    fr, fi = np.cos(ang) / 16.0, -np.sin(ang) / 16.0
    out = []
    for p in range(2):
        r, i = fr[:128, p::2], fi[:128, p::2]
        out.append(np.block([[r, -i], [i, r]]))
    for p in range(2):
        out.append(out[p].T)
    return np.stack(out).astype(ml_dtypes.bfloat16).astype(np.float32)


def dot(a, b):
    return jnp.dot(a, b, preferred_element_type=f32)


def remote(src, dst, sems, rems, i, dev):
    return pltpu.make_async_remote_copy(
        src_ref=src, dst_ref=dst, send_sem=sems.at[i], recv_sem=rems.at[i], device_id=dev, device_id_type=MESH
    )


def places():
    ty, tx = lax.axis_index("ty"), lax.axis_index("tx")
    left, right = (ty, lax.rem(tx + NX - 1, NX)), (ty, lax.rem(tx + 1, NX))
    above, below = (lax.rem(ty + NY - 1, NY), tx), (lax.rem(ty + 1, NY), tx)
    return ty, tx, left, right, above, below


def halo_kernel(
    spec_hbm, probe_hbm, tab_hbm, amp_hbm, ext_ref, split_ref, tab_out, amp_out, spec_ref, probe_ref, tab_ref, tmp, ls, ss, rs
):
    ty, tx, left, right, above, below = places()
    bar = pltpu.get_barrier_semaphore()
    for dev in (right, below):
        pl.semaphore_signal(bar, inc=1, device_id=dev, device_id_type=MESH)
    pairs = ((spec_hbm, spec_ref), (probe_hbm, probe_ref), (tab_hbm, tab_ref), (amp_hbm, amp_out))
    loads = [pltpu.make_async_copy(src, dst, ls.at[i]) for i, (src, dst) in enumerate(pairs)]
    for load in loads:
        load.start()
    pos = lax.broadcasted_iota(jnp.int32, (256, 256), 0)
    col = lax.broadcasted_iota(jnp.int32, (256, 256), 1)
    perm = ((col & 127) * 2 + (col >> 7) == pos).astype(f32).astype(bf16)
    loads[0].wait()
    for pln in range(2):
        w = dot(spec_ref[pln].astype(bf16), perm)
        tmp[pln, 0] = w[:, :128]
        tmp[pln, 1] = w[:, 128:]
    for pln in range(2):
        for rp in range(2):
            for cp in range(2):
                ext_ref[pln, rp, cp, 0, 0:256, :] = tmp[pln, cp, pl.ds(rp, 256, stride=2), :].astype(bf16)
    pl.semaphore_wait(bar, 2)
    top, own, low = slice(0, 128), slice(0, 256), slice(256, 384)

    def block(pln, ct, rows):
        return ext_ref.at[pln, :, :, ct, rows, :]

    a = remote(block(0, 0, top), block(0, 0, low), ss, rs, 0, above)
    c = remote(block(1, 0, top), block(1, 1, top), ss, rs, 1, left)
    b = remote(block(1, 0, top), block(1, 0, low), ss, rs, 2, above)
    d = remote(block(0, 0, own), block(0, 1, own), ss, rs, 3, left)
    e = remote(block(1, 0, slice(128, 256)), block(1, 1, slice(128, 256)), ss, rs, 4, left)
    corner0 = remote(block(0, 0, low), block(0, 1, low), ss, rs, 5, left)
    corner1_up = remote(block(1, 1, top), block(1, 1, low), ss, rs, 6, above)
    corner1_left = remote(block(1, 0, low), block(1, 1, low), ss, rs, 6, left)
    odd = lax.rem(tx, 2) == 1
    for copy in (a, c, b, d, e):
        copy.start()
    loads[1].wait()
    loads[2].wait()
    tab_out[...] = tab_ref[...].astype(bf16)
    for pln in range(2):
        value = probe_ref[pln]
        terms = 0.0
        for _ in range(3):
            part = value.astype(bf16)
            value = value - part.astype(f32)
            terms = terms + dot(part, perm)
        tmp[pln, 0, 0:256] = terms[:, :128]
        tmp[pln, 1, 0:256] = terms[:, 128:]
    for pln in range(2):
        for q in range(2):
            for cp in range(2):
                split_ref[pln, q, cp] = tmp[pln, cp, pl.ds(q, 128, stride=2), :]
    c.wait_recv()

    @pl.when(odd)
    def _():
        corner1_up.start()

    a.wait_recv()
    corner0.start()
    b.wait_recv()

    @pl.when(odd)
    def _():
        corner1_left.start()

    d.wait_recv()
    e.wait_recv()
    corner0.wait_recv()
    corner1_up.wait_recv()
    loads[3].wait()
    for copy in (a, c, b, d, e, corner0):
        copy.wait_send()

    @pl.when(odd)
    def _():
        corner1_up.wait_send()
        corner1_left.wait_send()


def pattern_kernel(first, n_ref, off_ref, ext_ref, *refs):
    if first:
        probe_ref, tab_ref, amp_ref, acc, mis_ref, obj, prol, macc, W, L, R, Y = refs
        obj[...] = ext_ref[...].astype(f32)
    else:
        tot_ref, alpha_ref, probe_ref, tab_ref, amp_ref, acc, mis_ref, obj, prol, macc, W, L, R, Y = refs
        obj[...] = ext_ref[...].astype(f32) - alpha_ref[0:1, :] * tot_ref[...]
    acc[...] = jnp.zeros_like(acc)
    macc[0] = jnp.zeros((8, 128), f32)
    lane = lax.broadcasted_iota(jnp.int32, (128, 128), 1)
    n = n_ref[0]
    halves = (slice(0, 128), slice(128, 256))

    def geometry(i):
        live = i < n
        s = jnp.minimum(i, n - 1)
        r = off_ref[0, s] & 511
        c = off_ref[1, s] & 255
        rho = r & 1
        start = (r >> 1, (r + rho) >> 1)
        masks = [lane * 2 + cp >= c for cp in range(2)]
        return live, s, c, start, (rho, 1 - rho), masks

    def make_wave(k, i):
        _, s, c, start, par, masks = geometry(i)
        for cp in range(2):
            pp = cp ^ (c & 1)
            shift = ((c + pp - cp) >> 1) & 127
            for q in range(2):
                sl = pl.ds(start[q], 128)
                p = [pltpu.roll(probe_ref[pln, q, pp], shift, 1) for pln in range(2)]
                o = [
                    jnp.where(masks[cp], obj[pln, par[q], cp, 0, sl, :], obj[pln, par[q], cp, 1, sl, :])
                    for pln in range(2)
                ]
                for pln in range(2):
                    prol[k, pln, q, cp] = p[pln]
                W[k, q, 0:128, halves[cp]] = (p[0] * o[0] - p[1] * o[1]).astype(bf16)
                W[k, q, 128:256, halves[cp]] = (p[0] * o[1] + p[1] * o[0]).astype(bf16)

    def rows_forward(k, i):
        t = [dot(tab_ref[q], W[k, q]) for q in range(2)]
        for h, near in enumerate(((t[0] + t[1]).astype(bf16), (t[0] - t[1]).astype(bf16))):
            for cp in range(2):
                L[k, cp, halves[h], 0:128] = near[:128, halves[cp]]
                L[k, cp, halves[h], 128:256] = near[128:, halves[cp]]

    def columns_forward(k, i):
        live, s, *_ = geometry(i)
        x = [dot(L[k, cp], tab_ref[2 + cp]) for cp in range(2)]
        res = []
        mis = jnp.zeros((8, 128), f32)
        for h in range(2):
            spectrum = x[0] + x[1] if h == 0 else x[0] - x[1]
            sr, si = spectrum[:, :128], spectrum[:, 128:]
            a = amp_ref[s, :, halves[h]].astype(f32)
            m2 = jnp.maximum(sr * sr + si * si, 1e-30)
            inv = lax.rsqrt(m2)
            dm = m2 * inv - a
            mis = mis + jnp.sum((dm * dm).reshape(32, 8, 128), axis=0)
            f = 1.0 - a * jnp.minimum(inv, FLOOR_INV)
            res.append((sr * f, si * f))
        macc[jnp.where(live, 0, 1)] += mis
        for pln in range(2):
            R[k, 0, :, halves[pln]] = (res[0][pln] + res[1][pln]).astype(bf16)
            R[k, 1, :, halves[pln]] = (res[0][pln] - res[1][pln]).astype(bf16)

    def columns_back(k, i):
        for cp in range(2):
            t = dot(R[k, cp], tab_ref[cp])
            for q in range(2):
                y = (t[:128] + t[128:] if q == 0 else t[:128] - t[128:]).astype(bf16)
                Y[k, q, 0:128, halves[cp]] = y[:, :128]
                Y[k, q, 128:256, halves[cp]] = y[:, 128:]

    def rows_back(k, i):
        live, s, c, start, par, masks = geometry(i)
        for q in range(2):
            z = dot(tab_ref[2 + q], Y[k, q])
            sl = pl.ds(jnp.where(live, start[q], 384), 128)
            for cp in range(2):
                pr, pi = prol[k, 0, q, cp], prol[k, 1, q, cp]
                zr, zi = z[:128, halves[cp]], z[128:, halves[cp]]
                grad = (pr * zr + pi * zi, pr * zi - pi * zr)
                for pln in range(2):
                    own = acc.at[pln, par[q], cp, 0, sl, :]
                    right = acc.at[pln, par[q], cp, 1, sl, :]
                    pltpu.store(own, own[...] + grad[pln], mask=masks[cp])
                    pltpu.store(right, right[...] + grad[pln], mask=jnp.logical_not(masks[cp]))

    stages = (make_wave, rows_forward, columns_forward, columns_back, rows_back)

    def group(j, _):
        for t in range(U + len(stages) - 1):
            for late, stage in enumerate(stages):
                if 0 <= t - late < U:
                    stage(t - late, j * U + t - late)
        return 0

    lax.fori_loop(0, (n + U - 1) // U, group, 0)
    mis_ref[...] = macc[0]


def group_barrier(ty, tx):
    bar = pltpu.get_barrier_semaphore()
    for k in [1, NY - 1] + list(range(2, NY - 1)):
        pl.semaphore_signal(bar, inc=1, device_id=(lax.rem(ty + k, NY), tx), device_id_type=MESH)
        if k in (1, NY - 1):
            x = 1 if k == 1 else NX - 1
            pl.semaphore_signal(bar, inc=1, device_id=(ty, lax.rem(tx + x, NX)), device_id_type=MESH)
    for k in range(2, NX - 1):
        pl.semaphore_signal(bar, inc=1, device_id=(ty, lax.rem(tx + k, NX)), device_id_type=MESH)
    return bar


def sum_vector(sq, mis):
    lane = lax.broadcasted_iota(jnp.int32, (1, 128), 1)
    sq = jnp.sum(sq, axis=0, keepdims=True)
    mis = jnp.sum(mis, axis=0, keepdims=True)
    return jnp.where(lane < 64, sq + pltpu.roll(sq, 64, 1), mis + pltpu.roll(mis, 64, 1))


def group_sum(vec, buf, ss, rs, me, size, device, beside=None):
    buf[me] = vec
    for k in range(1, size):
        remote_to(buf.at[me], buf.at[me], ss.at[0], rs.at[0], device(lax.rem(me + k, size))).start()
    if beside is not None:
        beside()
    rest = buf.at[pl.ds(0, size - 1)]
    every = remote_to(rest, rest, ss.at[0], rs.at[0], device(lax.rem(me + 1, size)))
    every.wait_recv()
    total = buf[0]
    for j in range(1, size):
        total = total + buf[j]
    return total, every


def all_sum(vec, ty, tx, ybuf, xbuf, ys, yr, xs, xr, beside=None):
    total, sent_y = group_sum(vec, ybuf, ys, yr, ty, NY, lambda j: (j, tx), beside)
    total, sent_x = group_sum(total, xbuf, xs, xr, tx, NX, lambda j: (ty, j))
    sent_y.wait_send()
    sent_x.wait_send()
    return total


def remote_to(src, dst, ssem, rsem, dev):
    return pltpu.make_async_remote_copy(
        src_ref=src, dst_ref=dst, send_sem=ssem, recv_sem=rsem, device_id=dev, device_id_type=MESH
    )


def half_sum(total, high):
    lane = lax.broadcasted_iota(jnp.int32, (1, 128), 1)
    return jnp.sum(jnp.where((lane >= 64) == high, total, 0.0), axis=1, keepdims=True)


def step_size(total):
    return RATE * lax.rsqrt(jnp.broadcast_to(half_sum(total, False) / AREA + EPS, (8, 128)))


SUM_SCRATCH = [
    pltpu.VMEM((NY, 1, 128), f32),
    pltpu.VMEM((NX, 1, 128), f32),
    pltpu.SemaphoreType.DMA((1,)),
    pltpu.SemaphoreType.DMA((1,)),
    pltpu.SemaphoreType.DMA((1,)),
    pltpu.SemaphoreType.DMA((1,)),
]
ENDS = (slice(0, 128), slice(256, 384))
MID = slice(128, 256)


def squares(value):
    return jnp.sum((value * value).reshape(-1, 8, 128), axis=0)


def spread_kernel(g_ref, mis_ref, tot_ref, sum_ref, alpha_ref, zsend, ysend, zrecv, yrecv, ss, rs, *sums):
    ty, tx, left, right, above, below = places()
    bar = group_barrier(ty, tx)

    def z(p, ct, rows, i):
        src, dst = zsend.at[p, ct, :, :, rows, :], zrecv.at[p, 1 - ct, :, :, rows, :]
        return remote(src, dst, ss, rs, 6 * p + 3 * ct + i, (left, right)[ct])

    def y(p, e, ct):
        return remote(ysend.at[p, e, ct], yrecv.at[p, 1 - e, ct], ss, rs, 12 + 4 * p + 2 * e + ct, (above, below)[e])

    for ct in (1, 0):
        for e in (1, 0):
            ysend[1, e, ct] = g_ref[1, :, :, ct, ENDS[e], :].astype(bf16)
    for e in (1, 0):
        for ct in (1, 0):
            zsend[0, ct, :, :, ENDS[e], :] = g_ref[0, :, :, ct, ENDS[e], :].astype(bf16)
    pl.semaphore_wait(bar, NY + NX - 2)
    for ct in (1, 0):
        for e in (1, 0):
            y(1, e, ct).start()
            z(0, ct, ENDS[e], e).start()
    for p in range(2):
        for ct in (1, 0):
            zsend[p, ct, :, :, MID, :] = g_ref[p, :, :, ct, MID, :].astype(bf16)
            z(p, ct, MID, 2).start()

    for ct in range(2):
        for e in (1, 0):
            z(0, 1 - ct, ENDS[e], e).wait_recv()
            value = g_ref[0, :, :, ct, ENDS[e], :] + zrecv[0, ct, :, :, ENDS[e], :].astype(f32)
            tot_ref[0, :, :, ct, ENDS[e], :] = value
            ysend[0, e, ct] = value.astype(bf16)
            if ct == 0:
                y(0, e, 0).start()
    for ct in (1, 0):
        for e in range(2):
            y(1, 1 - e, ct).wait_recv()
            value = g_ref[1, :, :, ct, ENDS[e], :] + yrecv[1, e, ct].astype(f32)
            tot_ref[1, :, :, ct, ENDS[e], :] = value
            zsend[1, ct, :, :, ENDS[e], :] = value.astype(bf16)
            z(1, ct, ENDS[e], e).start()
    for e in (1, 0):
        y(0, e, 1).start()
    sq = jnp.zeros((8, 128), f32)
    for p in range(2):
        z(p, 1, MID, 2).wait_recv()
        value = g_ref[p, :, :, 0, MID, :] + zrecv[p, 0, :, :, MID, :].astype(f32)
        tot_ref[p, :, :, 0, MID, :] = value
        sq = sq + squares(value)

    def add_y(e, ct):
        y(0, 1 - e, ct).wait_recv()
        value = tot_ref[0, :, :, ct, ENDS[e], :] + yrecv[0, e, ct].astype(f32)
        tot_ref[0, :, :, ct, ENDS[e], :] = value
        return value

    def add_z(e, ct):
        z(1, 1 - ct, ENDS[e], e).wait_recv()
        value = tot_ref[1, :, :, ct, ENDS[e], :] + zrecv[1, ct, :, :, ENDS[e], :].astype(f32)
        tot_ref[1, :, :, ct, ENDS[e], :] = value
        return value

    sq = sq + squares(add_z(0, 0))
    sq = sq + squares(add_y(0, 0))

    def beside():
        for p in range(2):
            z(p, 0, MID, 2).wait_recv()
            tot_ref[p, :, :, 1, MID, :] = g_ref[p, :, :, 1, MID, :] + zrecv[p, 1, :, :, MID, :].astype(f32)
        for e, ct in ((1, 0), (0, 1), (1, 1)):
            add_z(e, ct)
            add_y(e, ct)

    total = all_sum(sum_vector(sq, mis_ref[...]), ty, tx, *sums, beside=beside)
    sum_ref[...] = jnp.broadcast_to(total, (8, 128))
    alpha_ref[...] = step_size(total)
    for p in range(2):
        for ct in range(2):
            for e in range(2):
                y(p, e, ct).wait_send()
            for i, rows in enumerate(ENDS + (MID,)):
                z(p, ct, rows, i).wait_send()


def final_kernel(
    g_ref, mis_ref, tot_ref, sum_ref, alpha_ref, spec_ref, out_ref, misfit_ref, zsend, ysend, zrecv, yrecv, own, before, mixed, ss, rs, *sums
):
    ty, tx, left, right, above, below = places()
    bar = group_barrier(ty, tx)
    top, low, upper = ENDS[0], ENDS[1], slice(0, 256)
    for ct in (1, 0):
        ysend[1, ct] = g_ref[1, :, :, ct, low, :].astype(bf16)
    zsend[0, :, :, low, :] = g_ref[0, :, :, 1, low, :].astype(bf16)

    def z(p, rows, i):
        return remote(zsend.at[p, :, :, rows, :], zrecv.at[p, :, :, rows, :], ss, rs, i, right)

    def y(p, ct, i):
        return remote(ysend.at[p, ct], yrecv.at[p, ct], ss, rs, i, below)

    y1_right, y1_own, y0 = y(1, 1, 0), y(1, 0, 6), y(0, 0, 1)
    z0_low, z0_upper, z1_mid, z1_top = z(0, low, 2), z(0, upper, 3), z(1, MID, 4), z(1, top, 5)
    pl.semaphore_wait(bar, NY + NX - 2)
    y1_right.start()
    z0_low.start()
    y1_own.start()
    zsend[0, :, :, upper, :] = g_ref[0, :, :, 1, upper, :].astype(bf16)
    z0_upper.start()
    zsend[1, :, :, MID, :] = g_ref[1, :, :, 1, MID, :].astype(bf16)
    z1_mid.start()
    z0_low.wait_recv()
    ysend[0, 0] = (g_ref[0, :, :, 0, low, :] + zrecv[0, :, :, low, :].astype(f32)).astype(bf16)
    y0.start()
    y1_right.wait_recv()
    zsend[1, :, :, top, :] = (g_ref[1, :, :, 1, top, :] + yrecv[1, 1].astype(f32)).astype(bf16)
    z1_top.start()

    def interleave(value):
        pos = lax.broadcasted_iota(jnp.int32, (256, 256), 0)
        col = lax.broadcasted_iota(jnp.int32, (256, 256), 1)
        perm = ((pos & 127) * 2 + (pos >> 7) == col).astype(f32).astype(bf16)
        hi = value.astype(bf16)
        lo = (value - hi.astype(f32)).astype(bf16)
        return dot(hi, perm) + dot(lo, perm)

    def weave(dst, pln, value):
        for rp in range(2):
            w = interleave(jnp.concatenate([value[rp, 0], value[rp, 1]], axis=1))
            for h in range(2):
                dst[pln, h, pl.ds(rp, 256, stride=2), :] = w[:, h * 128 : h * 128 + 128]

    alpha = alpha_ref[0:1, :]
    for pln in range(2):
        weave(before, pln, alpha * tot_ref[pln, :, :, 0, upper, :])
    z0_upper.wait_recv()
    own[0, :, :, upper, :] = g_ref[0, :, :, 0, upper, :] + zrecv[0, :, :, upper, :].astype(f32)
    z1_mid.wait_recv()
    value = g_ref[1, :, :, 0, MID, :] + zrecv[1, :, :, MID, :].astype(f32)
    own[1, :, :, MID, :] = value
    sq = squares(value) + squares(own[0, :, :, MID, :])
    y1_own.wait_recv()
    z1_top.wait_recv()
    value = g_ref[1, :, :, 0, top, :] + yrecv[1, 0].astype(f32) + zrecv[1, :, :, top, :].astype(f32)
    own[1, :, :, top, :] = value
    sq = sq + squares(value)
    y0.wait_recv()
    value = own[0, :, :, top, :] + yrecv[0, 0].astype(f32)
    own[0, :, :, top, :] = value
    sq = sq + squares(value)

    def beside():
        for pln in range(2):
            weave(mixed, pln, own[pln])

    total = all_sum(sum_vector(sq, mis_ref[...]), ty, tx, *sums, beside=beside)
    alpha = step_size(total)[0:1, :]
    for pln in range(2):
        for h in range(2):
            cols = slice(h * 128, h * 128 + 128)
            out_ref[pln, :, cols] = spec_ref[pln, :, cols] - before[pln, h] - alpha * mixed[pln, h]
    misfit_ref[0] = half_sum(sum_ref[0:1, :], True)[0, 0] / MIS_TOTAL
    misfit_ref[1] = half_sum(total, True)[0, 0] / MIS_TOTAL
    for copy in (y1_right, y1_own, y0, z0_low, z0_upper, z1_mid, z1_top):
        copy.wait_send()


VM = pl.BlockSpec(memory_space=pltpu.VMEM)
SM = pl.BlockSpec(memory_space=pltpu.SMEM)


def params(mib, cid=None):
    if cid is None:
        return pltpu.CompilerParams(vmem_limit_bytes=mib << 20)
    return pltpu.CompilerParams(vmem_limit_bytes=mib << 20, collective_id=cid, has_side_effects=True)


def shape(dims, t):
    return jax.ShapeDtypeStruct(dims, t)


def patterns(first, *args):
    return pl.pallas_call(
        functools.partial(pattern_kernel, first),
        out_shape=(shape((2, 2, 2, 2, 512, 128), f32), shape((8, 128), f32)),
        in_specs=[SM, SM] + [VM] * (len(args) - 2),
        out_specs=(VM, VM),
        scratch_shapes=[
            pltpu.VMEM(EXT, f32),
            pltpu.VMEM((U, 2, 2, 2, 128, 128), f32),
            pltpu.VMEM((2, 8, 128), f32),
            *[pltpu.VMEM((U, 2, 256, 256), bf16)] * 4,
        ],
        compiler_params=params(28),
        name="patterns",
    )(*args)


def body(specimen, probe_wave, amplitudes, counts, offsets):
    off = offsets[0].T
    ext, probe, tab, amp = pl.pallas_call(
        halo_kernel,
        out_shape=(
            shape(EXT, bf16),
            shape((2, 2, 2, 128, 128), f32),
            shape((4, 256, 256), bf16),
            shape((24, 256, 256), bf16),
        ),
        in_specs=[pl.BlockSpec(memory_space=pltpu.HBM)] * 4,
        out_specs=(VM,) * 4,
        scratch_shapes=[
            pltpu.VMEM((2, 512, 256), f32),
            pltpu.VMEM((2, 256, 256), f32),
            pltpu.VMEM((4, 256, 256), f32),
            pltpu.VMEM((2, 2, 512, 128), f32),
            pltpu.SemaphoreType.DMA((4,)),
            pltpu.SemaphoreType.DMA((7,)),
            pltpu.SemaphoreType.DMA((7,)),
        ],
        compiler_params=params(16, 0),
        name="halo",
    )(*[pltpu.with_memory_space_constraint(x, pltpu.HBM) for x in (specimen, probe_wave, jnp.asarray(tables()), amplitudes[0])])
    g1, mis1 = patterns(True, counts, off, ext, probe, tab, amp)
    tot1, sum1, alpha1 = pl.pallas_call(
        spread_kernel,
        out_shape=(shape(EXT, f32), shape((8, 128), f32), shape((8, 128), f32)),
        in_specs=[VM] * 2,
        out_specs=(VM,) * 3,
        scratch_shapes=[
            pltpu.VMEM((2, 2, 2, 2, 384, 128), bf16),
            pltpu.VMEM((2, 2, 2, 2, 2, 128, 128), bf16),
            pltpu.VMEM((2, 2, 2, 2, 384, 128), bf16),
            pltpu.VMEM((2, 2, 2, 2, 2, 128, 128), bf16),
            pltpu.SemaphoreType.DMA((20,)),
            pltpu.SemaphoreType.DMA((20,)),
            *SUM_SCRATCH,
        ],
        compiler_params=params(16, 1),
        name="spread",
    )(g1, mis1)
    g2, mis2 = patterns(False, counts, off, ext, tot1, alpha1, probe, tab, amp)
    return pl.pallas_call(
        final_kernel,
        out_shape=(shape((2, 512, 256), f32), shape((2,), f32)),
        in_specs=[VM] * 6,
        out_specs=(VM, SM),
        scratch_shapes=[
            pltpu.VMEM((2, 2, 2, 384, 128), bf16),
            pltpu.VMEM((2, 2, 2, 2, 128, 128), bf16),
            pltpu.VMEM((2, 2, 2, 384, 128), bf16),
            pltpu.VMEM((2, 2, 2, 2, 128, 128), bf16),
            pltpu.VMEM((2, 2, 2, 256, 128), f32),
            pltpu.VMEM((2, 2, 512, 128), f32),
            pltpu.VMEM((2, 2, 512, 128), f32),
            pltpu.SemaphoreType.DMA((7,)),
            pltpu.SemaphoreType.DMA((7,)),
            *SUM_SCRATCH,
        ],
        compiler_params=params(16, 2),
        name="final",
    )(g2, mis2, tot1, sum1, alpha1, specimen)


def solution(mesh):
    return jax.shard_map(
        body,
        mesh=mesh,
        in_specs=(P(None, "ty", "tx"), P(), P(("ty", "tx"), None, None, None), P(("ty", "tx")), P(("ty", "tx"), None, None)),
        out_specs=(P(None, "ty", "tx"), P()),
        check_vma=False,
    )
```

```python
import functools

import jax
import jax.numpy as jnp
import ml_dtypes
import numpy as np
from jax import lax
from jax.experimental import pallas as pl
from jax.experimental.pallas import tpu as pltpu
from jax.sharding import PartitionSpec as P

MESH = pl.DeviceIdType.MESH
f32, bf16 = jnp.float32, jnp.bfloat16
NY, NX = 16, 8
ENDS = (slice(0, 128), slice(256, 384))
MID = slice(128, 256)
U = 4
EXT = (2, 2, 2, 2, 384, 128)
AREA = 8192.0 * 2048.0
RATE = 0.1
EPS = 1e-6
FLOOR_INV = 2.0
MIS_TOTAL = 1024.0 * 65536.0


def tables():
    n = 256
    k = np.arange(n)
    ang = (k[:, None] * k[None, :] % n) * (2 * np.pi / n)
    fr, fi = np.cos(ang) / 16.0, -np.sin(ang) / 16.0
    out = []
    for p in range(2):
        r, i = fr[:128, p::2], fi[:128, p::2]
        out.append(np.block([[r, -i], [i, r]]))
    for p in range(2):
        out.append(out[p].T)
    return np.stack(out).astype(ml_dtypes.bfloat16).astype(np.float32)


def dot(a, b):
    return jnp.dot(a, b, preferred_element_type=f32)


def remote(src, dst, sems, rems, i, dev):
    return pltpu.make_async_remote_copy(
        src_ref=src, dst_ref=dst, send_sem=sems.at[i], recv_sem=rems.at[i], device_id=dev, device_id_type=MESH
    )


def places():
    ty, tx = lax.axis_index("ty"), lax.axis_index("tx")
    left, right = (ty, lax.rem(tx + NX - 1, NX)), (ty, lax.rem(tx + 1, NX))
    above, below = (lax.rem(ty + NY - 1, NY), tx), (lax.rem(ty + 1, NY), tx)
    return ty, tx, left, right, above, below


def halo_kernel(
    spec_hbm, probe_hbm, tab_hbm, amp_hbm, ext_ref, split_ref, tab_out, amp_out, spec_ref, probe_ref, tab_ref, tmp, ls, ss, rs
):
    ty, tx, left, right, above, below = places()
    bar = pltpu.get_barrier_semaphore()
    for dev in (right, below):
        pl.semaphore_signal(bar, inc=1, device_id=dev, device_id_type=MESH)
    upper, lower = (slice(None), slice(0, 256)), (slice(None), slice(256, 512))
    pairs = ((spec_hbm.at[upper], spec_ref.at[upper]), (spec_hbm.at[lower], spec_ref.at[lower]), (probe_hbm, probe_ref), (tab_hbm, tab_ref), (amp_hbm, amp_out))
    loads = [pltpu.make_async_copy(src, dst, ls.at[i]) for i, (src, dst) in enumerate(pairs)]
    for load in loads:
        load.start()
    pos = lax.broadcasted_iota(jnp.int32, (256, 256), 0)
    col = lax.broadcasted_iota(jnp.int32, (256, 256), 1)
    perm = ((col & 127) * 2 + (col >> 7) == pos).astype(f32).astype(bf16)

    def split(rows):
        n = rows.stop - rows.start
        for pln in range(2):
            w = dot(spec_ref[pln, rows].astype(bf16), perm)
            tmp[pln, 0, rows] = w[:, :128]
            tmp[pln, 1, rows] = w[:, 128:]
        half = slice(rows.start // 2, rows.stop // 2)
        for pln in range(2):
            for rp in range(2):
                for cp in range(2):
                    odd_rows = tmp[pln, cp, pl.ds(rows.start + rp, n // 2, stride=2), :]
                    ext_ref[pln, rp, cp, 0, half, :] = odd_rows.astype(bf16)

    loads[0].wait()
    split(slice(0, 256))
    pl.semaphore_wait(bar, 2)
    top, low = ENDS

    def block(pln, ct, rows):
        return ext_ref.at[pln, :, :, ct, rows, :]

    a = remote(block(0, 0, top), block(0, 0, low), ss, rs, 0, above)
    c = remote(block(1, 0, top), block(1, 1, top), ss, rs, 1, left)
    b = remote(block(1, 0, top), block(1, 0, low), ss, rs, 2, above)
    d = remote(block(0, 0, top), block(0, 1, top), ss, rs, 3, left)
    e = [remote(block(p, 0, MID), block(p, 1, MID), ss, rs, (7, 4)[p], left) for p in range(2)]
    corner0 = remote(block(0, 0, low), block(0, 1, low), ss, rs, 5, left)
    corner1_up = remote(block(1, 1, top), block(1, 1, low), ss, rs, 6, above)
    corner1_left = remote(block(1, 0, low), block(1, 1, low), ss, rs, 6, left)
    odd = lax.rem(tx, 2) == 1
    for copy in (a, c, b, d):
        copy.start()
    loads[1].wait()
    split(slice(256, 512))
    for copy in e:
        copy.start()
    loads[2].wait()
    loads[3].wait()
    tab_out[...] = tab_ref[...].astype(bf16)
    for pln in range(2):
        value = probe_ref[pln]
        terms = 0.0
        for _ in range(3):
            part = value.astype(bf16)
            value = value - part.astype(f32)
            terms = terms + dot(part, perm)
        tmp[pln, 0, 0:256] = terms[:, :128]
        tmp[pln, 1, 0:256] = terms[:, 128:]
    for pln in range(2):
        for q in range(2):
            for cp in range(2):
                split_ref[pln, q, cp] = tmp[pln, cp, pl.ds(q, 128, stride=2), :]
    c.wait_recv()

    @pl.when(odd)
    def _():
        corner1_up.start()

    a.wait_recv()
    corner0.start()
    b.wait_recv()

    @pl.when(odd)
    def _():
        corner1_left.start()

    d.wait_recv()
    for copy in e:
        copy.wait_recv()
    corner0.wait_recv()
    corner1_up.wait_recv()
    loads[4].wait()
    for copy in (a, c, b, d, *e, corner0):
        copy.wait_send()

    @pl.when(odd)
    def _():
        corner1_up.wait_send()
        corner1_left.wait_send()


def pattern_kernel(first, n_ref, off_ref, ext_ref, *refs):
    if first:
        probe_ref, tab_ref, amp_ref, acc, mis_ref, obj, prol, macc, W, L, R, Y = refs
        obj[...] = ext_ref[...].astype(f32)
    else:
        tot_ref, alpha_ref, probe_ref, tab_ref, amp_ref, acc, mis_ref, obj, prol, macc, W, L, R, Y = refs
        obj[...] = ext_ref[...].astype(f32) - alpha_ref[0:1, :] * tot_ref[...]
    acc[...] = jnp.zeros_like(acc)
    macc[0] = jnp.zeros((8, 128), f32)
    lane = lax.broadcasted_iota(jnp.int32, (128, 128), 1)
    n = n_ref[0]
    halves = (slice(0, 128), slice(128, 256))

    def geometry(i):
        live = i < n
        s = jnp.minimum(i, n - 1)
        r = off_ref[0, s] & 511
        c = off_ref[1, s] & 255
        rho = r & 1
        start = (r >> 1, (r + rho) >> 1)
        masks = [lane * 2 + cp >= c for cp in range(2)]
        return live, s, c, start, (rho, 1 - rho), masks

    def make_wave(k, i):
        _, s, c, start, par, masks = geometry(i)
        for cp in range(2):
            pp = cp ^ (c & 1)
            shift = ((c + pp - cp) >> 1) & 127
            for q in range(2):
                sl = pl.ds(start[q], 128)
                p = [pltpu.roll(probe_ref[pln, q, pp], shift, 1) for pln in range(2)]
                o = [
                    jnp.where(masks[cp], obj[pln, par[q], cp, 0, sl, :], obj[pln, par[q], cp, 1, sl, :])
                    for pln in range(2)
                ]
                for pln in range(2):
                    prol[k, pln, q, cp] = p[pln]
                W[k, q, 0:128, halves[cp]] = (p[0] * o[0] - p[1] * o[1]).astype(bf16)
                W[k, q, 128:256, halves[cp]] = (p[0] * o[1] + p[1] * o[0]).astype(bf16)

    def rows_forward(k, i):
        t = [dot(tab_ref[q], W[k, q]) for q in range(2)]
        for h, near in enumerate(((t[0] + t[1]).astype(bf16), (t[0] - t[1]).astype(bf16))):
            for cp in range(2):
                L[k, cp, halves[h], 0:128] = near[:128, halves[cp]]
                L[k, cp, halves[h], 128:256] = near[128:, halves[cp]]

    def columns_forward(k, i):
        live, s, *_ = geometry(i)
        x = [dot(L[k, cp], tab_ref[2 + cp]) for cp in range(2)]
        res = []
        mis = jnp.zeros((8, 128), f32)
        for h in range(2):
            spectrum = x[0] + x[1] if h == 0 else x[0] - x[1]
            sr, si = spectrum[:, :128], spectrum[:, 128:]
            a = amp_ref[s, :, halves[h]].astype(f32)
            m2 = jnp.maximum(sr * sr + si * si, 1e-30)
            inv = lax.rsqrt(m2)
            dm = m2 * inv - a
            mis = mis + jnp.sum((dm * dm).reshape(32, 8, 128), axis=0)
            f = 1.0 - a * jnp.minimum(inv, FLOOR_INV)
            res.append((sr * f, si * f))
        macc[jnp.where(live, 0, 1)] += mis
        for pln in range(2):
            R[k, 0, :, halves[pln]] = (res[0][pln] + res[1][pln]).astype(bf16)
            R[k, 1, :, halves[pln]] = (res[0][pln] - res[1][pln]).astype(bf16)

    def columns_back(k, i):
        for cp in range(2):
            t = dot(R[k, cp], tab_ref[cp])
            for q in range(2):
                y = (t[:128] + t[128:] if q == 0 else t[:128] - t[128:]).astype(bf16)
                Y[k, q, 0:128, halves[cp]] = y[:, :128]
                Y[k, q, 128:256, halves[cp]] = y[:, 128:]

    def rows_back(k, i):
        live, s, c, start, par, masks = geometry(i)
        for q in range(2):
            z = dot(tab_ref[2 + q], Y[k, q])
            sl = pl.ds(jnp.where(live, start[q], 384), 128)
            for cp in range(2):
                pr, pi = prol[k, 0, q, cp], prol[k, 1, q, cp]
                zr, zi = z[:128, halves[cp]], z[128:, halves[cp]]
                grad = (pr * zr + pi * zi, pr * zi - pi * zr)
                for pln in range(2):
                    own = acc.at[pln, par[q], cp, 0, sl, :]
                    right = acc.at[pln, par[q], cp, 1, sl, :]
                    pltpu.store(own, own[...] + grad[pln], mask=masks[cp])
                    pltpu.store(right, right[...] + grad[pln], mask=jnp.logical_not(masks[cp]))

    stages = (make_wave, rows_forward, columns_forward, columns_back, rows_back)

    def group(j, _):
        for t in range(U + len(stages) - 1):
            for late, stage in enumerate(stages):
                if 0 <= t - late < U:
                    stage(t - late, j * U + t - late)
        return 0

    lax.fori_loop(0, (n + U - 1) // U, group, 0)
    mis_ref[...] = macc[0]


def group_barrier(ty, tx):
    bar = pltpu.get_barrier_semaphore()
    for k in [1, NY - 1] + list(range(2, NY - 1)):
        pl.semaphore_signal(bar, inc=1, device_id=(lax.rem(ty + k, NY), tx), device_id_type=MESH)
        if k in (1, NY - 1):
            x = 1 if k == 1 else NX - 1
            pl.semaphore_signal(bar, inc=1, device_id=(ty, lax.rem(tx + x, NX)), device_id_type=MESH)
    for k in range(2, NX - 1):
        pl.semaphore_signal(bar, inc=1, device_id=(ty, lax.rem(tx + k, NX)), device_id_type=MESH)
    return bar


def sum_vector(sq, mis):
    lane = lax.broadcasted_iota(jnp.int32, (1, 128), 1)
    sq = jnp.sum(sq, axis=0, keepdims=True)
    mis = jnp.sum(mis, axis=0, keepdims=True)
    return jnp.where(lane < 64, sq + pltpu.roll(sq, 64, 1), mis + pltpu.roll(mis, 64, 1))


def group_sum(vec, buf, ss, rs, me, size, device, beside):
    buf[me] = vec
    for k in range(1, size):
        remote_to(buf.at[me], buf.at[me], ss.at[0], rs.at[0], device(lax.rem(me + k, size))).start()
    beside()
    rest = buf.at[pl.ds(0, size - 1)]
    every = remote_to(rest, rest, ss.at[0], rs.at[0], device(lax.rem(me + 1, size)))
    every.wait_recv()
    total = buf[0]
    for j in range(1, size):
        total = total + buf[j]
    return total, every


def all_sum(vec, ty, tx, ybuf, xbuf, ys, yr, xs, xr, beside, later):
    total, sent_y = group_sum(vec, ybuf, ys, yr, ty, NY, lambda j: (j, tx), beside)
    total, sent_x = group_sum(total, xbuf, xs, xr, tx, NX, lambda j: (ty, j), later)
    sent_y.wait_send()
    sent_x.wait_send()
    return total


def remote_to(src, dst, ssem, rsem, dev):
    return pltpu.make_async_remote_copy(
        src_ref=src, dst_ref=dst, send_sem=ssem, recv_sem=rsem, device_id=dev, device_id_type=MESH
    )


def half_sum(total, high):
    lane = lax.broadcasted_iota(jnp.int32, (1, 128), 1)
    return jnp.sum(jnp.where((lane >= 64) == high, total, 0.0), axis=1, keepdims=True)


def step_size(total):
    return RATE * lax.rsqrt(jnp.broadcast_to(half_sum(total, False) / AREA + EPS, (8, 128)))


SUM_SCRATCH = [
    pltpu.VMEM((NY, 1, 128), f32),
    pltpu.VMEM((NX, 1, 128), f32),
    pltpu.SemaphoreType.DMA((1,)),
    pltpu.SemaphoreType.DMA((1,)),
    pltpu.SemaphoreType.DMA((1,)),
    pltpu.SemaphoreType.DMA((1,)),
]


def squares(value):
    return jnp.sum((value * value).reshape(-1, 8, 128), axis=0)


def spread_kernel(g_ref, mis_ref, tot_ref, sum_ref, alpha_ref, zsend, ysend, zrecv, yrecv, ss, rs, *sums):
    ty, tx, left, right, above, below = places()
    bar = group_barrier(ty, tx)
    odd = lax.rem(tx, 2) == 1
    pieces = ENDS + (MID,)

    def z(p, ct, i):
        src, dst = zsend.at[p, ct, :, :, pieces[i], :], zrecv.at[p, 1 - ct, :, :, pieces[i], :]
        return remote(src, dst, ss, rs, 6 * p + 3 * ct + i, (left, right)[ct])

    def y(p, e, ct):
        return remote(ysend.at[p, e, ct], yrecv.at[p, 1 - e, ct], ss, rs, 12 + 4 * p + 2 * e + ct, (above, below)[e])

    def put_z(p, ct, i, value):
        zsend[p, ct, :, :, pieces[i], :] = value.astype(bf16)
        z(p, ct, i).start()

    def put_y(p, e, ct, value):
        ysend[p, e, ct] = value.astype(bf16)
        y(p, e, ct).start()

    def got_z(p, ct, i):
        z(p, 1 - ct, i).wait_recv()
        return zrecv[p, ct, :, :, pieces[i], :].astype(f32)

    def got_y(p, e, ct):
        y(p, 1 - e, ct).wait_recv()
        return yrecv[p, e, ct].astype(f32)

    def raw(p, ct, i):
        return g_ref[p, :, :, ct, pieces[i], :]

    def keep(p, ct, i, value):
        tot_ref[p, :, :, ct, pieces[i], :] = value
        return value

    def kept(p, ct, i):
        return tot_ref[p, :, :, ct, pieces[i], :]

    pl.semaphore_wait(bar, NY + NX - 2)

    @pl.when(jnp.logical_not(odd))
    def _():
        for e in (1, 0):
            put_y(1, e, 0, raw(1, 0, e))
            for p in (1, 0):
                put_z(p, 1, e, raw(p, 1, e))
        for e in (1, 0):
            put_z(0, 0, e, raw(0, 0, e))
        for p in range(2):
            for ct in range(2):
                put_z(p, ct, 2, raw(p, ct, 2))
        for e in (1, 0):
            put_y(0, e, 0, keep(0, 0, e, raw(0, 0, e) + got_z(0, 0, e)))
        for e in (0, 1):
            put_z(1, 0, e, keep(1, 0, e, raw(1, 0, e) + got_y(1, e, 0)))
        for p in range(2):
            keep(p, 0, 2, raw(p, 0, 2) + got_z(p, 0, 2))
        keep(1, 0, 0, kept(1, 0, 0) + got_z(1, 0, 0))
        keep(0, 0, 0, kept(0, 0, 0) + got_y(0, 0, 0))

    @pl.when(odd)
    def _():
        for e in (1, 0):
            put_y(1, e, 1, raw(1, 1, e))
            put_z(0, 1, e, raw(0, 1, e))
        for p in (1, 0):
            for e in (1, 0):
                put_y(p, e, 0, keep(p, 0, e, raw(p, 0, e) + got_z(p, 0, e)))
        for p in range(2):
            put_z(p, 1, 2, raw(p, 1, 2))
        for e in (1, 0):
            put_y(0, e, 1, keep(0, 1, e, raw(0, 1, e) + got_z(0, 1, e)))
        for e in (0, 1):
            put_z(1, 1, e, keep(1, 1, e, raw(1, 1, e) + got_y(1, e, 1)))
        for p in range(2):
            keep(p, 0, 2, raw(p, 0, 2) + got_z(p, 0, 2))
        for p in (1, 0):
            keep(p, 0, 0, kept(p, 0, 0) + got_y(p, 0, 0))

    sq = squares(tot_ref[:, :, :, 0, 0:256, :])

    def beside():
        @pl.when(jnp.logical_not(odd))
        def _():
            keep(1, 0, 1, kept(1, 0, 1) + got_z(1, 0, 1))
            keep(0, 0, 1, kept(0, 0, 1) + got_y(0, 1, 0))

        @pl.when(odd)
        def _():
            for p in (1, 0):
                put_z(p, 0, 0, kept(p, 0, 0))
                put_z(p, 0, 2, kept(p, 0, 2))
            for p in (1, 0):
                put_z(p, 0, 1, keep(p, 0, 1, kept(p, 0, 1) + got_y(p, 1, 0)))
            for p in range(2):
                keep(p, 1, 2, raw(p, 1, 2) + got_z(p, 1, 2))
            for e in range(2):
                keep(0, 1, e, kept(0, 1, e) + got_y(0, e, 1))
                keep(1, 1, e, kept(1, 1, e) + got_z(1, 1, e))

    def later():
        @pl.when(jnp.logical_not(odd))
        def _():
            for i in (0, 2, 1):
                for p in (1, 0):
                    keep(p, 1, i, got_z(p, 1, i))

    total = all_sum(sum_vector(sq, mis_ref[...]), ty, tx, *sums, beside=beside, later=later)
    sum_ref[...] = jnp.broadcast_to(total, (8, 128))
    alpha_ref[...] = step_size(total)
    for p in range(2):
        for e in range(2):
            y(p, e, 0).wait_send()
        for ct in range(2):
            for i in range(3):
                z(p, ct, i).wait_send()

    @pl.when(odd)
    def _():
        for p in range(2):
            for e in range(2):
                y(p, e, 1).wait_send()


def final_kernel(
    g_ref, mis_ref, tot_ref, alpha_ref, before, mixed, sum_ref, zsend, ysend, zrecv, yrecv, own, ss, rs, *sums
):
    ty, tx, left, right, above, below = places()
    bar = group_barrier(ty, tx)
    odd = lax.rem(tx, 2) == 1
    pieces = ENDS + (MID,)

    def z(p, i):
        return remote(zsend.at[p, :, :, pieces[i], :], zrecv.at[p, :, :, pieces[i], :], ss, rs, 3 * p + i, right)

    def y(p, ct):
        return remote(ysend.at[p, ct], yrecv.at[p, ct], ss, rs, 6 + 2 * p + ct, below)

    def put_z(p, i, value):
        zsend[p, :, :, pieces[i], :] = value.astype(bf16)
        z(p, i).start()

    def put_y(p, ct, value):
        ysend[p, ct] = value.astype(bf16)
        y(p, ct).start()

    def got_z(p, i):
        z(p, i).wait_recv()
        return zrecv[p, :, :, pieces[i], :].astype(f32)

    def got_y(p, ct):
        y(p, ct).wait_recv()
        return yrecv[p, ct].astype(f32)

    def raw(p, ct, i):
        return g_ref[p, :, :, ct, pieces[i], :]

    pl.semaphore_wait(bar, NY + NX - 2)

    @pl.when(jnp.logical_not(odd))
    def _():
        put_y(1, 0, raw(1, 0, 1))
        for p, i in ((1, 1), (0, 1), (1, 0), (0, 0), (1, 2), (0, 2)):
            put_z(p, i, raw(p, 1, i))
        put_y(0, 0, raw(0, 0, 1) + got_z(0, 1))

    @pl.when(odd)
    def _():
        put_y(1, 1, raw(1, 1, 1))
        put_z(0, 1, raw(0, 1, 1))
        for p in (1, 0):
            put_y(p, 0, raw(p, 0, 1) + got_z(p, 1))
        put_z(0, 0, raw(0, 1, 0))
        put_z(1, 2, raw(1, 1, 2))
        put_z(0, 2, raw(0, 1, 2))
        put_z(1, 0, raw(1, 1, 0) + got_y(1, 1))

    sq = jnp.zeros((8, 128), f32)
    for p in range(2):
        value = raw(p, 0, 2) + got_z(p, 2)
        own[p, :, :, MID, :] = value
        sq = sq + squares(value)
    for p in (1, 0):
        value = raw(p, 0, 0) + got_y(p, 0) + got_z(p, 0)
        own[p, :, :, ENDS[0], :] = value
        sq = sq + squares(value)
    pos = lax.broadcasted_iota(jnp.int32, (256, 256), 0)
    col = lax.broadcasted_iota(jnp.int32, (256, 256), 1)
    perm = ((pos & 127) * 2 + (pos >> 7) == col).astype(f32).astype(bf16)

    def weave(dst, pln, value):
        for rp in range(2):
            rest = jnp.concatenate([value[rp, 0], value[rp, 1]], axis=1)
            hi = rest.astype(bf16)
            lo = (rest - hi.astype(f32)).astype(bf16)
            w = dot(hi, perm) + dot(lo, perm)
            for h in range(2):
                dst[pln, h, pl.ds(rp, 256, stride=2), :] = w[:, h * 128 : h * 128 + 128]

    def beside():
        for pln in range(2):
            weave(mixed, pln, own[pln])

    def later():
        for pln in range(2):
            weave(before, pln, alpha_ref[0:1, :] * tot_ref[pln, :, :, 0, 0:256, :])

    total = all_sum(sum_vector(sq, mis_ref[...]), ty, tx, *sums, beside=beside, later=later)
    sum_ref[...] = jnp.broadcast_to(total, (8, 128))
    for p in range(2):
        for i in (0, 2):
            z(p, i).wait_send()
        y(p, 0).wait_send()
    z(0, 1).wait_send()

    @pl.when(odd)
    def _():
        y(1, 1).wait_send()

    @pl.when(jnp.logical_not(odd))
    def _():
        z(1, 1).wait_send()


def finish_kernel(spec_ref, before, mixed, sum1_ref, sum2_ref, out_ref, misfit_ref, new, sems):
    alpha = step_size(sum2_ref[0:1, :])[0:1, :]
    copies = []
    for pln in range(2):
        for h in range(2):
            cols = slice(h * 128, h * 128 + 128)
            new[pln, :, cols] = spec_ref[pln, :, cols] - before[pln, h] - alpha * mixed[pln, h]
        copies.append(pltpu.make_async_copy(new.at[pln], out_ref.at[pln], sems.at[pln]))
        copies[-1].start()
    misfit_ref[0] = half_sum(sum1_ref[0:1, :], True)[0, 0] / MIS_TOTAL
    misfit_ref[1] = half_sum(sum2_ref[0:1, :], True)[0, 0] / MIS_TOTAL
    for copy in copies:
        copy.wait()


VM = pl.BlockSpec(memory_space=pltpu.VMEM)
SM = pl.BlockSpec(memory_space=pltpu.SMEM)


def params(mib, cid=None):
    if cid is None:
        return pltpu.CompilerParams(vmem_limit_bytes=mib << 20)
    return pltpu.CompilerParams(vmem_limit_bytes=mib << 20, collective_id=cid, has_side_effects=True)


def shape(dims, t):
    return jax.ShapeDtypeStruct(dims, t)


def patterns(first, *args):
    return pl.pallas_call(
        functools.partial(pattern_kernel, first),
        out_shape=(shape((2, 2, 2, 2, 512, 128), f32), shape((8, 128), f32)),
        in_specs=[SM, SM] + [VM] * (len(args) - 2),
        out_specs=(VM, VM),
        scratch_shapes=[
            pltpu.VMEM(EXT, f32),
            pltpu.VMEM((U, 2, 2, 2, 128, 128), f32),
            pltpu.VMEM((2, 8, 128), f32),
            *[pltpu.VMEM((U, 2, 256, 256), bf16)] * 4,
        ],
        compiler_params=params(28),
        name="patterns",
    )(*args)


def body(specimen, probe_wave, amplitudes, counts, offsets):
    off = offsets[0].T
    ext, probe, tab, amp = pl.pallas_call(
        halo_kernel,
        out_shape=(
            shape(EXT, bf16),
            shape((2, 2, 2, 128, 128), f32),
            shape((4, 256, 256), bf16),
            shape((24, 256, 256), bf16),
        ),
        in_specs=[pl.BlockSpec(memory_space=pltpu.HBM)] * 4,
        out_specs=(VM,) * 4,
        scratch_shapes=[
            pltpu.VMEM((2, 512, 256), f32),
            pltpu.VMEM((2, 256, 256), f32),
            pltpu.VMEM((4, 256, 256), f32),
            pltpu.VMEM((2, 2, 512, 128), f32),
            pltpu.SemaphoreType.DMA((5,)),
            pltpu.SemaphoreType.DMA((8,)),
            pltpu.SemaphoreType.DMA((8,)),
        ],
        compiler_params=params(16, 0),
        name="halo",
    )(*[pltpu.with_memory_space_constraint(x, pltpu.HBM) for x in (specimen, probe_wave, jnp.asarray(tables()), amplitudes[0])])
    g1, mis1 = patterns(True, counts, off, ext, probe, tab, amp)
    tot1, sum1, alpha1 = pl.pallas_call(
        spread_kernel,
        out_shape=(shape(EXT, f32), shape((8, 128), f32), shape((8, 128), f32)),
        in_specs=[VM] * 2,
        out_specs=(VM,) * 3,
        scratch_shapes=[
            pltpu.VMEM((2, 2, 2, 2, 384, 128), bf16),
            pltpu.VMEM((2, 2, 2, 2, 2, 128, 128), bf16),
            pltpu.VMEM((2, 2, 2, 2, 384, 128), bf16),
            pltpu.VMEM((2, 2, 2, 2, 2, 128, 128), bf16),
            pltpu.SemaphoreType.DMA((20,)),
            pltpu.SemaphoreType.DMA((20,)),
            *SUM_SCRATCH,
        ],
        compiler_params=params(16, 1),
        name="spread",
    )(g1, mis1)
    g2, mis2 = patterns(False, counts, off, ext, tot1, alpha1, probe, tab, amp)
    before, mixed, sum2 = pl.pallas_call(
        final_kernel,
        out_shape=(shape((2, 2, 512, 128), f32), shape((2, 2, 512, 128), f32), shape((8, 128), f32)),
        in_specs=[VM] * 4,
        out_specs=(VM,) * 3,
        scratch_shapes=[
            pltpu.VMEM((2, 2, 2, 384, 128), bf16),
            pltpu.VMEM((2, 2, 2, 2, 128, 128), bf16),
            pltpu.VMEM((2, 2, 2, 384, 128), bf16),
            pltpu.VMEM((2, 2, 2, 2, 128, 128), bf16),
            pltpu.VMEM((2, 2, 2, 256, 128), f32),
            pltpu.SemaphoreType.DMA((10,)),
            pltpu.SemaphoreType.DMA((10,)),
            *SUM_SCRATCH,
        ],
        compiler_params=params(16, 2),
        name="final",
    )(g2, mis2, tot1, alpha1)
    return pl.pallas_call(
        finish_kernel,
        out_shape=(shape((2, 512, 256), f32), shape((2,), f32)),
        in_specs=[VM] * 5,
        out_specs=(pl.BlockSpec(memory_space=pl.ANY), SM),
        scratch_shapes=[pltpu.VMEM((2, 512, 256), f32), pltpu.SemaphoreType.DMA((2,))],
        compiler_params=params(16),
        name="finish",
    )(specimen, before, mixed, sum1, sum2)


def solution(mesh):
    return jax.shard_map(
        body,
        mesh=mesh,
        in_specs=(P(None, "ty", "tx"), P(), P(("ty", "tx"), None, None, None), P(("ty", "tx")), P(("ty", "tx"), None, None)),
        out_specs=(P(None, "ty", "tx"), P()),
        check_vma=False,
    )
```

```python
import functools

import jax
import jax.numpy as jnp
import ml_dtypes
import numpy as np
from jax import lax
from jax.experimental import pallas as pl
from jax.experimental.pallas import tpu as pltpu
from jax.sharding import PartitionSpec as P

MESH = pl.DeviceIdType.MESH
f32, bf16 = jnp.float32, jnp.bfloat16
NY, NX = 16, 8
ENDS = (slice(0, 128), slice(256, 384))
MID = slice(128, 256)
U = 6
KEEP = 6
ROWS = 32
EXT = (2, 2, 2, 2, 384, 128)
AREA = 8192.0 * 2048.0
RATE = 0.1
EPS = 1e-6
FLOOR_INV = 2.0
MIS_TOTAL = 1024.0 * 65536.0


def tables():
    n = 256
    k = np.arange(n)
    ang = (k[:, None] * k[None, :] % n) * (2 * np.pi / n)
    fr, fi = np.cos(ang) / 16.0, -np.sin(ang) / 16.0
    out = []
    for p in range(2):
        r, i = fr[:128, p::2], fi[:128, p::2]
        out.append(np.block([[r, -i], [i, r]]))
    for p in range(2):
        out.append(out[p].T)
    return np.stack(out).astype(ml_dtypes.bfloat16).astype(np.float32)


def dot(a, b):
    return jnp.dot(a, b, preferred_element_type=f32)


def remote(src, dst, sems, rems, i, dev):
    return pltpu.make_async_remote_copy(
        src_ref=src, dst_ref=dst, send_sem=sems.at[i], recv_sem=rems.at[i], device_id=dev, device_id_type=MESH
    )


def places():
    ty, tx = lax.axis_index("ty"), lax.axis_index("tx")
    left, right = (ty, lax.rem(tx + NX - 1, NX)), (ty, lax.rem(tx + 1, NX))
    above, below = (lax.rem(ty + NY - 1, NY), tx), (lax.rem(ty + 1, NY), tx)
    return ty, tx, left, right, above, below


def halo_kernel(
    spec_hbm, probe_hbm, tab_hbm, amp_hbm, ext_ref, split_ref, tab_out, amp_out, spec_ref, probe_ref, tab_ref, tmp, ls, ss, rs
):
    ty, tx, left, right, above, below = places()
    bar = pltpu.get_barrier_semaphore()
    for dev in (right, below):
        pl.semaphore_signal(bar, inc=1, device_id=dev, device_id_type=MESH)
    upper, lower = (slice(None), slice(0, 256)), (slice(None), slice(256, 512))
    pairs = ((spec_hbm.at[upper], spec_ref.at[upper]), (spec_hbm.at[lower], spec_ref.at[lower]), (probe_hbm, probe_ref), (tab_hbm, tab_ref), (amp_hbm, amp_out))
    loads = [pltpu.make_async_copy(src, dst, ls.at[i]) for i, (src, dst) in enumerate(pairs)]
    for load in loads:
        load.start()
    pos = lax.broadcasted_iota(jnp.int32, (256, 256), 0)
    col = lax.broadcasted_iota(jnp.int32, (256, 256), 1)
    perm = ((col & 127) * 2 + (col >> 7) == pos).astype(f32).astype(bf16)

    def split(rows):
        n = rows.stop - rows.start
        for pln in range(2):
            w = dot(spec_ref[pln, rows].astype(bf16), perm)
            tmp[pln, 0, rows] = w[:, :128]
            tmp[pln, 1, rows] = w[:, 128:]
        half = slice(rows.start // 2, rows.stop // 2)
        for pln in range(2):
            for rp in range(2):
                for cp in range(2):
                    odd_rows = tmp[pln, cp, pl.ds(rows.start + rp, n // 2, stride=2), :]
                    ext_ref[pln, rp, cp, 0, half, :] = odd_rows.astype(bf16)

    loads[0].wait()
    split(slice(0, 256))
    pl.semaphore_wait(bar, 2)
    top, low = ENDS

    def block(pln, ct, rows):
        return ext_ref.at[pln, :, :, ct, rows, :]

    a = remote(block(0, 0, top), block(0, 0, low), ss, rs, 0, above)
    c = remote(block(1, 0, top), block(1, 1, top), ss, rs, 1, left)
    b = remote(block(1, 0, top), block(1, 0, low), ss, rs, 2, above)
    d = remote(block(0, 0, top), block(0, 1, top), ss, rs, 3, left)
    e = [remote(block(p, 0, MID), block(p, 1, MID), ss, rs, (7, 4)[p], left) for p in range(2)]
    corner0 = remote(block(0, 0, low), block(0, 1, low), ss, rs, 5, left)
    corner1_up = remote(block(1, 1, top), block(1, 1, low), ss, rs, 6, above)
    corner1_left = remote(block(1, 0, low), block(1, 1, low), ss, rs, 6, left)
    odd = lax.rem(tx, 2) == 1
    for copy in (a, c, b, d):
        copy.start()
    loads[1].wait()
    split(slice(256, 512))
    for copy in e:
        copy.start()
    loads[2].wait()
    loads[3].wait()
    tab_out[...] = tab_ref[...].astype(bf16)
    for pln in range(2):
        value = probe_ref[pln]
        terms = 0.0
        for _ in range(3):
            part = value.astype(bf16)
            value = value - part.astype(f32)
            terms = terms + dot(part, perm)
        tmp[pln, 0, 0:256] = terms[:, :128]
        tmp[pln, 1, 0:256] = terms[:, 128:]
    for pln in range(2):
        for q in range(2):
            for cp in range(2):
                split_ref[pln, q, cp] = tmp[pln, cp, pl.ds(q, 128, stride=2), :]
    c.wait_recv()

    @pl.when(odd)
    def _():
        corner1_up.start()

    a.wait_recv()
    corner0.start()
    b.wait_recv()

    @pl.when(odd)
    def _():
        corner1_left.start()

    d.wait_recv()
    for copy in e:
        copy.wait_recv()
    corner0.wait_recv()
    corner1_up.wait_recv()
    loads[4].wait()
    for copy in (a, c, b, d, *e, corner0):
        copy.wait_send()

    @pl.when(odd)
    def _():
        corner1_up.wait_send()
        corner1_left.wait_send()


def pattern_kernel(first, n_ref, off_ref, ext_ref, *refs):
    if first:
        probe_ref, tab_ref, amp_ref, acc, mis_ref, obj, prol, macc, W, L, R, Y = refs
        obj[...] = ext_ref[...].astype(f32)
    else:
        tot_ref, alpha_ref, probe_ref, tab_ref, amp_ref, acc, mis_ref, obj, prol, macc, W, L, R, Y = refs
        obj[...] = ext_ref[...].astype(f32) - alpha_ref[0:1, :] * tot_ref[...]
    acc[:, :, :, :, 0:384, :] = jnp.zeros(EXT, f32)
    macc[0] = jnp.zeros((8, 128), f32)
    lane = lax.broadcasted_iota(jnp.int32, (128, 128), 1)
    n = n_ref[0]
    halves = (slice(0, 128), slice(128, 256))

    def geometry(i):
        live = i < n
        s = jnp.minimum(i, n - 1)
        r = off_ref[0, s] & 511
        c = off_ref[1, s] & 255
        rho = r & 1
        start = (r >> 1, (r + rho) >> 1)
        masks = [lane * 2 + cp >= c for cp in range(2)]
        return live, s, c, start, (rho, 1 - rho), masks

    def make_wave(k, i):
        _, s, c, start, par, masks = geometry(i)
        for cp in range(2):
            pp = cp ^ (c & 1)
            shift = ((c + pp - cp) >> 1) & 127
            for q in range(2):
                sl = pl.ds(start[q], 128)
                p = [pltpu.roll(probe_ref[pln, q, pp], shift, 1) for pln in range(2)]
                o = [
                    jnp.where(masks[cp], obj[pln, par[q], cp, 0, sl, :], obj[pln, par[q], cp, 1, sl, :])
                    for pln in range(2)
                ]
                for pln in range(2):
                    prol[k, pln, q, cp] = p[pln]
                W[k, q, 0:128, halves[cp]] = (p[0] * o[0] - p[1] * o[1]).astype(bf16)
                W[k, q, 128:256, halves[cp]] = (p[0] * o[1] + p[1] * o[0]).astype(bf16)

    def products(accs):
        state = dict(staged=0, half=0, waiting=None)
        count = 256 // ROWS

        def take():
            if state["waiting"] is not None:
                state["waiting"]()
            state["waiting"] = None

        def start(weights, lhs, use):
            staged, base = state["staged"], state["half"] * count
            state["staged"], state["half"] = 1 - staged, 1 - state["half"]
            for unit in range(2):
                pltpu.matmul_push_rhs(weights[unit], staged, unit)
            for j in range(count):
                for unit in range(2):
                    pltpu.matmul_acc_lhs(accs[unit][base + j], lhs(unit, j), staged if j == 0 else None)
            take()

            def results():
                for j in range(count):
                    use(j, pltpu.matmul_pop(accs[0][base + j]), pltpu.matmul_pop(accs[1][base + j]))

            state["waiting"] = results

        return start, take

    def run(*accs):
        half = len(accs) // 2
        start, take = products((accs[:half], accs[half:]))

        def rows_forward(k, i):
            def use(j, t0, t1):
                pln, u = j * ROWS // 128, j * ROWS % 128
                for h, near in enumerate(((t0 + t1).astype(bf16), (t0 - t1).astype(bf16))):
                    for cp in range(2):
                        L[k, cp, 128 * h + u : 128 * h + u + ROWS, halves[pln]] = near[:, halves[cp]]

            start([W[k, 0], W[k, 1]], lambda unit, j: tab_ref[unit, j * ROWS : (j + 1) * ROWS], use)

        def columns_forward(k, i):
            live, s, *_ = geometry(i)
            mis = [jnp.zeros((8, 128), f32)]

            def use(j, x0, x1):
                rows = slice(j * ROWS, (j + 1) * ROWS)
                res = []
                for h in range(2):
                    spectrum = x0 + x1 if h == 0 else x0 - x1
                    sr, si = spectrum[:, :128], spectrum[:, 128:]
                    a = amp_ref[s, rows, halves[h]].astype(f32)
                    m2 = jnp.maximum(sr * sr + si * si, 1e-30)
                    inv = lax.rsqrt(m2)
                    dm = m2 * inv - a
                    mis[0] = mis[0] + jnp.sum((dm * dm).reshape(ROWS // 8, 8, 128), axis=0)
                    f = 1.0 - a * jnp.minimum(inv, FLOOR_INV)
                    res.append((sr * f, si * f))
                for pln in range(2):
                    R[k, 0, rows, halves[pln]] = (res[0][pln] + res[1][pln]).astype(bf16)
                    R[k, 1, rows, halves[pln]] = (res[0][pln] - res[1][pln]).astype(bf16)
                if j == 256 // ROWS - 1:
                    macc[jnp.where(live, 0, 1)] += mis[0]

            start([tab_ref[2], tab_ref[3]], lambda unit, j: L[k, unit, j * ROWS : (j + 1) * ROWS], use)

        def two_rows(ref, j):
            h = ROWS // 2
            return jnp.concatenate([ref[j * h : (j + 1) * h], ref[128 + j * h : 128 + (j + 1) * h]], axis=0)

        def columns_back(k, i):
            h = ROWS // 2

            def use(j, *terms):
                for cp, t in enumerate(terms):
                    for q in range(2):
                        y = (t[:h] + t[h:] if q == 0 else t[:h] - t[h:]).astype(bf16)
                        Y[k, q, j * h : (j + 1) * h, halves[cp]] = y[:, :128]
                        Y[k, q, 128 + j * h : 128 + (j + 1) * h, halves[cp]] = y[:, 128:]

            start([tab_ref[0], tab_ref[1]], lambda unit, j: two_rows(R.at[k, unit], j), use)

        def rows_back(k, i):
            live, s, c, first_row, par, masks = geometry(i)
            h = ROWS // 2

            def use(j, *terms):
                for q, t in enumerate(terms):
                    sl = pl.ds(jnp.where(live, first_row[q], 384) + j * h, h)
                    rows = slice(j * h, (j + 1) * h)
                    for cp in range(2):
                        pr, pi = prol[k, 0, q, cp, rows], prol[k, 1, q, cp, rows]
                        zr, zi = t[:h, halves[cp]], t[h:, halves[cp]]
                        grad = (pr * zr + pi * zi, pr * zi - pi * zr)
                        mask = masks[cp][:h]
                        for pln in range(2):
                            own = acc.at[pln, par[q], cp, 0, sl, :]
                            right = acc.at[pln, par[q], cp, 1, sl, :]
                            pltpu.store(own, own[...] + grad[pln], mask=mask)
                            pltpu.store(right, right[...] + grad[pln], mask=jnp.logical_not(mask))

            start([Y[k, 0], Y[k, 1]], lambda unit, j: two_rows(tab_ref.at[2 + unit], j), use)

        stages = (make_wave, rows_forward, columns_forward, columns_back, rows_back)

        def group(j, _):
            for t in range(U + len(stages) - 1):
                for late, stage in enumerate(stages):
                    if 0 <= t - late < U:
                        stage((t - late) % KEEP, j * U + t - late)
            take()
            return 0

        lax.fori_loop(0, (n + U - 1) // U, group, 0)

    accumulators = 2 * 256 // ROWS
    pl.run_scoped(
        run,
        *[pltpu.ACC(mxu_id=0)((ROWS, 256), f32)] * accumulators,
        *[pltpu.ACC(mxu_id=1)((ROWS, 256), f32)] * accumulators,
    )
    mis_ref[...] = macc[0]


def group_barrier(ty, tx):
    bar = pltpu.get_barrier_semaphore()
    for k in [1, NY - 1] + list(range(2, NY - 1)):
        pl.semaphore_signal(bar, inc=1, device_id=(lax.rem(ty + k, NY), tx), device_id_type=MESH)
        if k in (1, NY - 1):
            x = 1 if k == 1 else NX - 1
            pl.semaphore_signal(bar, inc=1, device_id=(ty, lax.rem(tx + x, NX)), device_id_type=MESH)
    for k in range(2, NX - 1):
        pl.semaphore_signal(bar, inc=1, device_id=(ty, lax.rem(tx + k, NX)), device_id_type=MESH)
    return bar


def sum_vector(sq, mis):
    lane = lax.broadcasted_iota(jnp.int32, (1, 128), 1)
    sq = jnp.sum(sq, axis=0, keepdims=True)
    mis = jnp.sum(mis, axis=0, keepdims=True)
    return jnp.where(lane < 64, sq + pltpu.roll(sq, 64, 1), mis + pltpu.roll(mis, 64, 1))


def group_sum(vec, buf, ss, rs, me, size, device, beside):
    buf[me] = vec
    for k in range(1, size):
        remote_to(buf.at[me], buf.at[me], ss.at[0], rs.at[0], device(lax.rem(me + k, size))).start()
    beside()
    rest = buf.at[pl.ds(0, size - 1)]
    every = remote_to(rest, rest, ss.at[0], rs.at[0], device(lax.rem(me + 1, size)))
    every.wait_recv()
    total = buf[0]
    for j in range(1, size):
        total = total + buf[j]
    return total, every


def all_sum(vec, ty, tx, ybuf, xbuf, ys, yr, xs, xr, beside, later):
    total, sent_y = group_sum(vec, ybuf, ys, yr, ty, NY, lambda j: (j, tx), beside)
    total, sent_x = group_sum(total, xbuf, xs, xr, tx, NX, lambda j: (ty, j), later)
    sent_y.wait_send()
    sent_x.wait_send()
    return total


def remote_to(src, dst, ssem, rsem, dev):
    return pltpu.make_async_remote_copy(
        src_ref=src, dst_ref=dst, send_sem=ssem, recv_sem=rsem, device_id=dev, device_id_type=MESH
    )


def half_sum(total, high):
    lane = lax.broadcasted_iota(jnp.int32, (1, 128), 1)
    return jnp.sum(jnp.where((lane >= 64) == high, total, 0.0), axis=1, keepdims=True)


def step_size(total):
    return RATE * lax.rsqrt(jnp.broadcast_to(half_sum(total, False) / AREA + EPS, (8, 128)))


SUM_SCRATCH = [
    pltpu.VMEM((NY, 1, 128), f32),
    pltpu.VMEM((NX, 1, 128), f32),
    pltpu.SemaphoreType.DMA((1,)),
    pltpu.SemaphoreType.DMA((1,)),
    pltpu.SemaphoreType.DMA((1,)),
    pltpu.SemaphoreType.DMA((1,)),
]


def squares(value):
    return jnp.sum((value * value).reshape(-1, 8, 128), axis=0)


def spread_kernel(g_ref, mis_ref, tot_ref, sum_ref, alpha_ref, zsend, ysend, zrecv, yrecv, ss, rs, *sums):
    ty, tx, left, right, above, below = places()
    bar = group_barrier(ty, tx)
    odd = lax.rem(tx, 2) == 1
    pieces = ENDS + (MID,)

    def z(p, ct, i):
        src, dst = zsend.at[p, ct, :, :, pieces[i], :], zrecv.at[p, 1 - ct, :, :, pieces[i], :]
        return remote(src, dst, ss, rs, 6 * p + 3 * ct + i, (left, right)[ct])

    def y(p, e, ct):
        return remote(ysend.at[p, e, ct], yrecv.at[p, 1 - e, ct], ss, rs, 12 + 4 * p + 2 * e + ct, (above, below)[e])

    def put_z(p, ct, i, value):
        zsend[p, ct, :, :, pieces[i], :] = value.astype(bf16)
        z(p, ct, i).start()

    def put_y(p, e, ct, value):
        ysend[p, e, ct] = value.astype(bf16)
        y(p, e, ct).start()

    def got_z(p, ct, i):
        z(p, 1 - ct, i).wait_recv()
        return zrecv[p, ct, :, :, pieces[i], :].astype(f32)

    def got_y(p, e, ct):
        y(p, 1 - e, ct).wait_recv()
        return yrecv[p, e, ct].astype(f32)

    def raw(p, ct, i):
        return g_ref[p, :, :, ct, pieces[i], :]

    def keep(p, ct, i, value):
        tot_ref[p, :, :, ct, pieces[i], :] = value
        return value

    def kept(p, ct, i):
        return tot_ref[p, :, :, ct, pieces[i], :]

    pl.semaphore_wait(bar, NY + NX - 2)

    @pl.when(jnp.logical_not(odd))
    def _():
        for e in (1, 0):
            put_y(1, e, 0, raw(1, 0, e))
            for p in (1, 0):
                put_z(p, 1, e, raw(p, 1, e))
        for e in (1, 0):
            put_z(0, 0, e, raw(0, 0, e))
        for p in range(2):
            for ct in range(2):
                put_z(p, ct, 2, raw(p, ct, 2))
        for e in (1, 0):
            put_y(0, e, 0, keep(0, 0, e, raw(0, 0, e) + got_z(0, 0, e)))
        for e in (0, 1):
            put_z(1, 0, e, keep(1, 0, e, raw(1, 0, e) + got_y(1, e, 0)))
        for p in range(2):
            keep(p, 0, 2, raw(p, 0, 2) + got_z(p, 0, 2))
        keep(1, 0, 0, kept(1, 0, 0) + got_z(1, 0, 0))
        keep(0, 0, 0, kept(0, 0, 0) + got_y(0, 0, 0))

    @pl.when(odd)
    def _():
        for e in (1, 0):
            put_y(1, e, 1, raw(1, 1, e))
            put_z(0, 1, e, raw(0, 1, e))
        for p in (1, 0):
            for e in (1, 0):
                put_y(p, e, 0, keep(p, 0, e, raw(p, 0, e) + got_z(p, 0, e)))
        for p in range(2):
            put_z(p, 1, 2, raw(p, 1, 2))
        for e in (1, 0):
            put_y(0, e, 1, keep(0, 1, e, raw(0, 1, e) + got_z(0, 1, e)))
        for e in (0, 1):
            put_z(1, 1, e, keep(1, 1, e, raw(1, 1, e) + got_y(1, e, 1)))
        for p in range(2):
            keep(p, 0, 2, raw(p, 0, 2) + got_z(p, 0, 2))
        for p in (1, 0):
            keep(p, 0, 0, kept(p, 0, 0) + got_y(p, 0, 0))

    sq = squares(tot_ref[:, :, :, 0, 0:256, :])

    def beside():
        @pl.when(jnp.logical_not(odd))
        def _():
            keep(1, 0, 1, kept(1, 0, 1) + got_z(1, 0, 1))
            keep(0, 0, 1, kept(0, 0, 1) + got_y(0, 1, 0))

        @pl.when(odd)
        def _():
            for p in (1, 0):
                put_z(p, 0, 0, kept(p, 0, 0))
                put_z(p, 0, 2, kept(p, 0, 2))
            for p in (1, 0):
                put_z(p, 0, 1, keep(p, 0, 1, kept(p, 0, 1) + got_y(p, 1, 0)))
            for p in range(2):
                keep(p, 1, 2, raw(p, 1, 2) + got_z(p, 1, 2))
            for e in range(2):
                keep(0, 1, e, kept(0, 1, e) + got_y(0, e, 1))
                keep(1, 1, e, kept(1, 1, e) + got_z(1, 1, e))

    def later():
        @pl.when(jnp.logical_not(odd))
        def _():
            for i in (0, 2, 1):
                for p in (1, 0):
                    keep(p, 1, i, got_z(p, 1, i))

    total = all_sum(sum_vector(sq, mis_ref[...]), ty, tx, *sums, beside=beside, later=later)
    sum_ref[...] = jnp.broadcast_to(total, (8, 128))
    alpha_ref[...] = step_size(total)
    for p in range(2):
        for e in range(2):
            y(p, e, 0).wait_send()
        for ct in range(2):
            for i in range(3):
                z(p, ct, i).wait_send()

    @pl.when(odd)
    def _():
        for p in range(2):
            for e in range(2):
                y(p, e, 1).wait_send()


def final_kernel(
    g_ref, mis_ref, tot_ref, alpha_ref, before, mixed, sum_ref, zsend, ysend, zrecv, yrecv, own, ss, rs, *sums
):
    ty, tx, left, right, above, below = places()
    bar = group_barrier(ty, tx)
    odd = lax.rem(tx, 2) == 1
    pieces = ENDS + (MID,)

    def z(p, i):
        return remote(zsend.at[p, :, :, pieces[i], :], zrecv.at[p, :, :, pieces[i], :], ss, rs, 3 * p + i, right)

    def y(p, ct):
        return remote(ysend.at[p, ct], yrecv.at[p, ct], ss, rs, 6 + 2 * p + ct, below)

    def put_z(p, i, value):
        zsend[p, :, :, pieces[i], :] = value.astype(bf16)
        z(p, i).start()

    def put_y(p, ct, value):
        ysend[p, ct] = value.astype(bf16)
        y(p, ct).start()

    def got_z(p, i):
        z(p, i).wait_recv()
        return zrecv[p, :, :, pieces[i], :].astype(f32)

    def got_y(p, ct):
        y(p, ct).wait_recv()
        return yrecv[p, ct].astype(f32)

    def raw(p, ct, i):
        return g_ref[p, :, :, ct, pieces[i], :]

    pl.semaphore_wait(bar, NY + NX - 2)

    @pl.when(jnp.logical_not(odd))
    def _():
        put_y(1, 0, raw(1, 0, 1))
        for p, i in ((1, 1), (0, 1), (1, 0), (0, 0), (1, 2), (0, 2)):
            put_z(p, i, raw(p, 1, i))
        put_y(0, 0, raw(0, 0, 1) + got_z(0, 1))

    @pl.when(odd)
    def _():
        put_y(1, 1, raw(1, 1, 1))
        put_z(0, 1, raw(0, 1, 1))
        for p in (1, 0):
            put_y(p, 0, raw(p, 0, 1) + got_z(p, 1))
        put_z(0, 0, raw(0, 1, 0))
        put_z(1, 2, raw(1, 1, 2))
        put_z(0, 2, raw(0, 1, 2))
        put_z(1, 0, raw(1, 1, 0) + got_y(1, 1))

    sq = jnp.zeros((8, 128), f32)
    for p in range(2):
        value = raw(p, 0, 2) + got_z(p, 2)
        own[p, :, :, MID, :] = value
        sq = sq + squares(value)
    for p in (1, 0):
        value = raw(p, 0, 0) + got_y(p, 0) + got_z(p, 0)
        own[p, :, :, ENDS[0], :] = value
        sq = sq + squares(value)
    pos = lax.broadcasted_iota(jnp.int32, (256, 256), 0)
    col = lax.broadcasted_iota(jnp.int32, (256, 256), 1)
    perm = ((pos & 127) * 2 + (pos >> 7) == col).astype(f32).astype(bf16)

    def weave(dst, pln, value):
        for rp in range(2):
            rest = jnp.concatenate([value[rp, 0], value[rp, 1]], axis=1)
            hi = rest.astype(bf16)
            lo = (rest - hi.astype(f32)).astype(bf16)
            w = dot(hi, perm) + dot(lo, perm)
            for h in range(2):
                dst[pln, h, pl.ds(rp, 256, stride=2), :] = w[:, h * 128 : h * 128 + 128]

    def beside():
        for pln in range(2):
            weave(mixed, pln, own[pln])

    def later():
        for pln in range(2):
            weave(before, pln, alpha_ref[0:1, :] * tot_ref[pln, :, :, 0, 0:256, :])

    total = all_sum(sum_vector(sq, mis_ref[...]), ty, tx, *sums, beside=beside, later=later)
    sum_ref[...] = jnp.broadcast_to(total, (8, 128))
    for p in range(2):
        for i in (0, 2):
            z(p, i).wait_send()
        y(p, 0).wait_send()
    z(0, 1).wait_send()

    @pl.when(odd)
    def _():
        y(1, 1).wait_send()

    @pl.when(jnp.logical_not(odd))
    def _():
        z(1, 1).wait_send()


def finish_kernel(spec_ref, before, mixed, sum1_ref, sum2_ref, out_ref, misfit_ref, new, sems):
    alpha = step_size(sum2_ref[0:1, :])[0:1, :]
    copies = []
    for pln in range(2):
        for part in range(2):
            rows = slice(256 * part, 256 * part + 256)
            for h in range(2):
                cols = slice(h * 128, h * 128 + 128)
                new[pln, rows, cols] = spec_ref[pln, rows, cols] - before[pln, h, rows] - alpha * mixed[pln, h, rows]
            copies.append(pltpu.make_async_copy(new.at[pln, rows], out_ref.at[pln, rows], sems.at[2 * pln + part]))
            copies[-1].start()
    misfit_ref[0] = half_sum(sum1_ref[0:1, :], True)[0, 0] / MIS_TOTAL
    misfit_ref[1] = half_sum(sum2_ref[0:1, :], True)[0, 0] / MIS_TOTAL
    for copy in copies:
        copy.wait()


VM = pl.BlockSpec(memory_space=pltpu.VMEM)
SM = pl.BlockSpec(memory_space=pltpu.SMEM)


def params(mib, cid=None):
    if cid is None:
        return pltpu.CompilerParams(vmem_limit_bytes=mib << 20)
    return pltpu.CompilerParams(vmem_limit_bytes=mib << 20, collective_id=cid, has_side_effects=True)


def shape(dims, t):
    return jax.ShapeDtypeStruct(dims, t)


def patterns(first, *args):
    return pl.pallas_call(
        functools.partial(pattern_kernel, first),
        out_shape=(shape((2, 2, 2, 2, 512, 128), f32), shape((8, 128), f32)),
        in_specs=[SM, SM] + [VM] * (len(args) - 2),
        out_specs=(VM, VM),
        scratch_shapes=[
            pltpu.VMEM(EXT, f32),
            pltpu.VMEM((KEEP, 2, 2, 2, 128, 128), f32),
            pltpu.VMEM((2, 8, 128), f32),
            *[pltpu.VMEM((KEEP, 2, 256, 256), bf16)] * 4,
        ],
        compiler_params=params(28),
        name="patterns",
    )(*args)


def body(specimen, probe_wave, amplitudes, counts, offsets):
    off = offsets[0].T
    ext, probe, tab, amp = pl.pallas_call(
        halo_kernel,
        out_shape=(
            shape(EXT, bf16),
            shape((2, 2, 2, 128, 128), f32),
            shape((4, 256, 256), bf16),
            shape((24, 256, 256), bf16),
        ),
        in_specs=[pl.BlockSpec(memory_space=pltpu.HBM)] * 4,
        out_specs=(VM,) * 4,
        scratch_shapes=[
            pltpu.VMEM((2, 512, 256), f32),
            pltpu.VMEM((2, 256, 256), f32),
            pltpu.VMEM((4, 256, 256), f32),
            pltpu.VMEM((2, 2, 512, 128), f32),
            pltpu.SemaphoreType.DMA((5,)),
            pltpu.SemaphoreType.DMA((8,)),
            pltpu.SemaphoreType.DMA((8,)),
        ],
        compiler_params=params(16, 0),
        name="halo",
    )(*[pltpu.with_memory_space_constraint(x, pltpu.HBM) for x in (specimen, probe_wave, jnp.asarray(tables()), amplitudes[0])])
    g1, mis1 = patterns(True, counts, off, ext, probe, tab, amp)
    tot1, sum1, alpha1 = pl.pallas_call(
        spread_kernel,
        out_shape=(shape(EXT, f32), shape((8, 128), f32), shape((8, 128), f32)),
        in_specs=[VM] * 2,
        out_specs=(VM,) * 3,
        scratch_shapes=[
            pltpu.VMEM((2, 2, 2, 2, 384, 128), bf16),
            pltpu.VMEM((2, 2, 2, 2, 2, 128, 128), bf16),
            pltpu.VMEM((2, 2, 2, 2, 384, 128), bf16),
            pltpu.VMEM((2, 2, 2, 2, 2, 128, 128), bf16),
            pltpu.SemaphoreType.DMA((20,)),
            pltpu.SemaphoreType.DMA((20,)),
            *SUM_SCRATCH,
        ],
        compiler_params=params(16, 1),
        name="spread",
    )(g1, mis1)
    g2, mis2 = patterns(False, counts, off, ext, tot1, alpha1, probe, tab, amp)
    before, mixed, sum2 = pl.pallas_call(
        final_kernel,
        out_shape=(shape((2, 2, 512, 128), f32), shape((2, 2, 512, 128), f32), shape((8, 128), f32)),
        in_specs=[VM] * 4,
        out_specs=(VM,) * 3,
        scratch_shapes=[
            pltpu.VMEM((2, 2, 2, 384, 128), bf16),
            pltpu.VMEM((2, 2, 2, 2, 128, 128), bf16),
            pltpu.VMEM((2, 2, 2, 384, 128), bf16),
            pltpu.VMEM((2, 2, 2, 2, 128, 128), bf16),
            pltpu.VMEM((2, 2, 2, 256, 128), f32),
            pltpu.SemaphoreType.DMA((10,)),
            pltpu.SemaphoreType.DMA((10,)),
            *SUM_SCRATCH,
        ],
        compiler_params=params(16, 2),
        name="final",
    )(g2, mis2, tot1, alpha1)
    return pl.pallas_call(
        finish_kernel,
        out_shape=(shape((2, 512, 256), f32), shape((2,), f32)),
        in_specs=[VM] * 5,
        out_specs=(pl.BlockSpec(memory_space=pl.ANY), SM),
        scratch_shapes=[pltpu.VMEM((2, 512, 256), f32), pltpu.SemaphoreType.DMA((4,))],
        compiler_params=params(16),
        name="finish",
    )(specimen, before, mixed, sum1, sum2)


def solution(mesh):
    return jax.shard_map(
        body,
        mesh=mesh,
        in_specs=(P(None, "ty", "tx"), P(), P(("ty", "tx"), None, None, None), P(("ty", "tx")), P(("ty", "tx"), None, None)),
        out_specs=(P(None, "ty", "tx"), P()),
        check_vma=False,
    )
```

```python
import functools

import jax
import jax.numpy as jnp
import ml_dtypes
import numpy as np
from jax import lax
from jax.experimental import pallas as pl
from jax.experimental.pallas import tpu as pltpu
from jax.sharding import PartitionSpec as P

MESH = pl.DeviceIdType.MESH
f32, bf16 = jnp.float32, jnp.bfloat16
NY, NX = 16, 8
ENDS = (slice(0, 128), slice(256, 384))
MID = slice(128, 256)
U = 6
KEEP = 6
ROWS = 32
EXT = (2, 2, 2, 2, 384, 128)
AREA = 8192.0 * 2048.0
RATE = 0.1
EPS = 1e-6
FLOOR_INV = 2.0
MIS_TOTAL = 1024.0 * 65536.0


def tables():
    n = 256
    k = np.arange(n)
    ang = (k[:, None] * k[None, :] % n) * (2 * np.pi / n)
    fr, fi = np.cos(ang) / 16.0, -np.sin(ang) / 16.0
    out = []
    for p in range(2):
        r, i = fr[:128, p::2], fi[:128, p::2]
        out.append(np.block([[r, -i], [i, r]]))
    for p in range(2):
        out.append(out[p].T)
    return np.stack(out).astype(ml_dtypes.bfloat16).astype(np.float32)


def dot(a, b):
    return jnp.dot(a, b, preferred_element_type=f32)


def remote(src, dst, sems, rems, i, dev):
    return pltpu.make_async_remote_copy(
        src_ref=src, dst_ref=dst, send_sem=sems.at[i], recv_sem=rems.at[i], device_id=dev, device_id_type=MESH
    )


def places():
    ty, tx = lax.axis_index("ty"), lax.axis_index("tx")
    left, right = (ty, lax.rem(tx + NX - 1, NX)), (ty, lax.rem(tx + 1, NX))
    above, below = (lax.rem(ty + NY - 1, NY), tx), (lax.rem(ty + 1, NY), tx)
    return ty, tx, left, right, above, below


def halo_kernel(
    spec_hbm, probe_hbm, tab_hbm, amp_hbm, ext_ref, split_ref, tab_out, amp_out, zeros_ref, spec_ref, probe_ref, tab_ref, tmp, ls, ss, rs
):
    ty, tx, left, right, above, below = places()
    bar = pltpu.get_barrier_semaphore()
    for dev in (right, below):
        pl.semaphore_signal(bar, inc=1, device_id=dev, device_id_type=MESH)
    upper, lower = (slice(None), slice(0, 256)), (slice(None), slice(256, 512))
    pairs = ((spec_hbm.at[upper], spec_ref.at[upper]), (spec_hbm.at[lower], spec_ref.at[lower]), (probe_hbm, probe_ref), (tab_hbm, tab_ref), (amp_hbm, amp_out))
    loads = [pltpu.make_async_copy(src, dst, ls.at[i]) for i, (src, dst) in enumerate(pairs)]
    for load in loads:
        load.start()
    pos = lax.broadcasted_iota(jnp.int32, (256, 256), 0)
    col = lax.broadcasted_iota(jnp.int32, (256, 256), 1)
    perm = ((col & 127) * 2 + (col >> 7) == pos).astype(f32).astype(bf16)

    def split(rows):
        n = rows.stop - rows.start
        for pln in range(2):
            w = dot(spec_ref[pln, rows].astype(bf16), perm)
            tmp[pln, 0, rows] = w[:, :128]
            tmp[pln, 1, rows] = w[:, 128:]
        half = slice(rows.start // 2, rows.stop // 2)
        for pln in range(2):
            for rp in range(2):
                for cp in range(2):
                    odd_rows = tmp[pln, cp, pl.ds(rows.start + rp, n // 2, stride=2), :]
                    ext_ref[pln, rp, cp, 0, half, :] = odd_rows.astype(bf16)

    loads[0].wait()
    split(slice(0, 256))
    pl.semaphore_wait(bar, 2)
    top, low = ENDS

    def block(pln, ct, rows):
        return ext_ref.at[pln, :, :, ct, rows, :]

    a = remote(block(0, 0, top), block(0, 0, low), ss, rs, 0, above)
    c = remote(block(1, 0, top), block(1, 1, top), ss, rs, 1, left)
    b = remote(block(1, 0, top), block(1, 0, low), ss, rs, 2, above)
    d = remote(block(0, 0, top), block(0, 1, top), ss, rs, 3, left)
    e = [remote(block(p, 0, MID), block(p, 1, MID), ss, rs, (7, 4)[p], left) for p in range(2)]
    corner0 = remote(block(0, 0, low), block(0, 1, low), ss, rs, 5, left)
    corner1_up = remote(block(1, 1, top), block(1, 1, low), ss, rs, 6, above)
    corner1_left = remote(block(1, 0, low), block(1, 1, low), ss, rs, 6, left)
    odd = lax.rem(tx, 2) == 1
    for copy in (a, c, b, d):
        copy.start()
    loads[1].wait()
    split(slice(256, 512))
    for copy in e:
        copy.start()
    loads[2].wait()
    loads[3].wait()
    tab_out[...] = tab_ref[...].astype(bf16)
    for pln in range(2):
        value = probe_ref[pln]
        terms = 0.0
        for _ in range(3):
            part = value.astype(bf16)
            value = value - part.astype(f32)
            terms = terms + dot(part, perm)
        tmp[pln, 0, 0:256] = terms[:, :128]
        tmp[pln, 1, 0:256] = terms[:, 128:]
    for pln in range(2):
        for q in range(2):
            for cp in range(2):
                split_ref[pln, q, cp] = tmp[pln, cp, pl.ds(q, 128, stride=2), :]
    zeros_ref[...] = jnp.zeros_like(zeros_ref)
    c.wait_recv()

    @pl.when(odd)
    def _():
        corner1_up.start()

    a.wait_recv()
    corner0.start()
    b.wait_recv()

    @pl.when(odd)
    def _():
        corner1_left.start()

    d.wait_recv()
    for copy in e:
        copy.wait_recv()
    corner0.wait_recv()
    corner1_up.wait_recv()
    loads[4].wait()
    for copy in (a, c, b, d, *e, corner0):
        copy.wait_send()

    @pl.when(odd)
    def _():
        corner1_up.wait_send()
        corner1_left.wait_send()


def pattern_kernel(first, n_ref, off_hbm, zeros_ref, ext_ref, *refs):
    *refs, off_ref, sems = refs
    load = pltpu.make_async_copy(off_hbm, off_ref, sems.at[0])
    load.start()
    if first:
        probe_ref, tab_ref, amp_ref, acc, mis_ref, obj, prol, macc, W, L, R, Y = refs
        obj[...] = ext_ref[...].astype(f32)
    else:
        tot_ref, alpha_ref, probe_ref, tab_ref, amp_ref, acc, mis_ref, obj, prol, macc, W, L, R, Y = refs
        obj[...] = ext_ref[...].astype(f32) - alpha_ref[0:1, :] * tot_ref[...]
    macc[0] = jnp.zeros((8, 128), f32)
    lane = lax.broadcasted_iota(jnp.int32, (128, 128), 1)
    load.wait()
    n = n_ref[0]
    halves = (slice(0, 128), slice(128, 256))

    def geometry(i):
        live = i < n
        s = jnp.minimum(i, n - 1)
        r = off_ref[0, s] & 511
        c = off_ref[1, s] & 255
        rho = r & 1
        start = (r >> 1, (r + rho) >> 1)
        masks = [lane * 2 + cp >= c for cp in range(2)]
        return live, s, c, start, (rho, 1 - rho), masks

    def make_wave(k, i):
        _, s, c, start, par, masks = geometry(i)
        for cp in range(2):
            pp = cp ^ (c & 1)
            shift = ((c + pp - cp) >> 1) & 127
            for q in range(2):
                sl = pl.ds(start[q], 128)
                p = [pltpu.roll(probe_ref[pln, q, pp], shift, 1) for pln in range(2)]
                o = [
                    jnp.where(masks[cp], obj[pln, par[q], cp, 0, sl, :], obj[pln, par[q], cp, 1, sl, :])
                    for pln in range(2)
                ]
                for pln in range(2):
                    prol[k, pln, q, cp] = p[pln]
                W[k, q, 0:128, halves[cp]] = (p[0] * o[0] - p[1] * o[1]).astype(bf16)
                W[k, q, 128:256, halves[cp]] = (p[0] * o[1] + p[1] * o[0]).astype(bf16)

    def products(accs):
        state = dict(staged=0, half=0, waiting=None)
        count = 256 // ROWS

        def take():
            if state["waiting"] is not None:
                state["waiting"]()
            state["waiting"] = None

        def start(weights, lhs, use):
            staged, base = state["staged"], state["half"] * count
            state["staged"], state["half"] = 1 - staged, 1 - state["half"]
            for unit in range(2):
                pltpu.matmul_push_rhs(weights[unit], staged, unit)
            for j in range(count):
                for unit in range(2):
                    pltpu.matmul_acc_lhs(accs[unit][base + j], lhs(unit, j), staged if j == 0 else None)
            take()

            def results():
                for j in range(count):
                    use(j, pltpu.matmul_pop(accs[0][base + j]), pltpu.matmul_pop(accs[1][base + j]))

            state["waiting"] = results

        return start, take

    def run(*accs):
        half = len(accs) // 2
        start, take = products((accs[:half], accs[half:]))

        def rows_forward(k, i):
            def use(j, t0, t1):
                pln, u = j * ROWS // 128, j * ROWS % 128
                for h, near in enumerate(((t0 + t1).astype(bf16), (t0 - t1).astype(bf16))):
                    for cp in range(2):
                        L[k, cp, 128 * h + u : 128 * h + u + ROWS, halves[pln]] = near[:, halves[cp]]

            start([W[k, 0], W[k, 1]], lambda unit, j: tab_ref[unit, j * ROWS : (j + 1) * ROWS], use)

        def columns_forward(k, i):
            live, s, *_ = geometry(i)
            mis = [jnp.zeros((8, 128), f32)]

            def use(j, x0, x1):
                rows = slice(j * ROWS, (j + 1) * ROWS)
                res = []
                for h in range(2):
                    spectrum = x0 + x1 if h == 0 else x0 - x1
                    sr, si = spectrum[:, :128], spectrum[:, 128:]
                    a = amp_ref[s, rows, halves[h]].astype(f32)
                    m2 = jnp.maximum(sr * sr + si * si, 1e-30)
                    inv = lax.rsqrt(m2)
                    dm = m2 * inv - a
                    mis[0] = mis[0] + jnp.sum((dm * dm).reshape(ROWS // 8, 8, 128), axis=0)
                    f = 1.0 - a * jnp.minimum(inv, FLOOR_INV)
                    res.append((sr * f, si * f))
                for pln in range(2):
                    R[k, 0, rows, halves[pln]] = (res[0][pln] + res[1][pln]).astype(bf16)
                    R[k, 1, rows, halves[pln]] = (res[0][pln] - res[1][pln]).astype(bf16)
                if j == 256 // ROWS - 1:
                    macc[jnp.where(live, 0, 1)] += mis[0]

            start([tab_ref[2], tab_ref[3]], lambda unit, j: L[k, unit, j * ROWS : (j + 1) * ROWS], use)

        def two_rows(ref, j):
            h = ROWS // 2
            return jnp.concatenate([ref[j * h : (j + 1) * h], ref[128 + j * h : 128 + (j + 1) * h]], axis=0)

        def columns_back(k, i):
            h = ROWS // 2

            def use(j, *terms):
                for cp, t in enumerate(terms):
                    for q in range(2):
                        y = (t[:h] + t[h:] if q == 0 else t[:h] - t[h:]).astype(bf16)
                        Y[k, q, j * h : (j + 1) * h, halves[cp]] = y[:, :128]
                        Y[k, q, 128 + j * h : 128 + (j + 1) * h, halves[cp]] = y[:, 128:]

            start([tab_ref[0], tab_ref[1]], lambda unit, j: two_rows(R.at[k, unit], j), use)

        def rows_back(k, i):
            live, s, c, first_row, par, masks = geometry(i)
            h = ROWS // 2

            def use(j, *terms):
                for q, t in enumerate(terms):
                    sl = pl.ds(jnp.where(live, first_row[q], 384) + j * h, h)
                    rows = slice(j * h, (j + 1) * h)
                    for cp in range(2):
                        pr, pi = prol[k, 0, q, cp, rows], prol[k, 1, q, cp, rows]
                        zr, zi = t[:h, halves[cp]], t[h:, halves[cp]]
                        grad = (pr * zr + pi * zi, pr * zi - pi * zr)
                        mask = masks[cp][:h]
                        for pln in range(2):
                            own = acc.at[pln, par[q], cp, 0, sl, :]
                            right = acc.at[pln, par[q], cp, 1, sl, :]
                            pltpu.store(own, own[...] + grad[pln], mask=mask)
                            pltpu.store(right, right[...] + grad[pln], mask=jnp.logical_not(mask))

            start([Y[k, 0], Y[k, 1]], lambda unit, j: two_rows(tab_ref.at[2 + unit], j), use)

        stages = (make_wave, rows_forward, columns_forward, columns_back, rows_back)

        def group(j, _):
            for t in range(U + len(stages) - 1):
                for late, stage in enumerate(stages):
                    if 0 <= t - late < U:
                        stage((t - late) % KEEP, j * U + t - late)
            take()
            return 0

        lax.fori_loop(0, (n + U - 1) // U, group, 0)

    accumulators = 2 * 256 // ROWS
    pl.run_scoped(
        run,
        *[pltpu.ACC(mxu_id=0)((ROWS, 256), f32)] * accumulators,
        *[pltpu.ACC(mxu_id=1)((ROWS, 256), f32)] * accumulators,
    )
    mis_ref[...] = macc[0]


def group_barrier(ty, tx):
    bar = pltpu.get_barrier_semaphore()
    for k in [1, NY - 1] + list(range(2, NY - 1)):
        pl.semaphore_signal(bar, inc=1, device_id=(lax.rem(ty + k, NY), tx), device_id_type=MESH)
        if k in (1, NY - 1):
            x = 1 if k == 1 else NX - 1
            pl.semaphore_signal(bar, inc=1, device_id=(ty, lax.rem(tx + x, NX)), device_id_type=MESH)
    for k in range(2, NX - 1):
        pl.semaphore_signal(bar, inc=1, device_id=(ty, lax.rem(tx + k, NX)), device_id_type=MESH)
    return bar


def sum_vector(sq, mis):
    lane = lax.broadcasted_iota(jnp.int32, (1, 128), 1)
    sq = jnp.sum(sq, axis=0, keepdims=True)
    mis = jnp.sum(mis, axis=0, keepdims=True)
    return jnp.where(lane < 64, sq + pltpu.roll(sq, 64, 1), mis + pltpu.roll(mis, 64, 1))


def group_sum(vec, buf, ss, rs, me, size, device, beside):
    buf[me] = vec
    for k in range(1, size):
        remote_to(buf.at[me], buf.at[me], ss.at[0], rs.at[0], device(lax.rem(me + k, size))).start()
    beside()
    rest = buf.at[pl.ds(0, size - 1)]
    every = remote_to(rest, rest, ss.at[0], rs.at[0], device(lax.rem(me + 1, size)))
    every.wait_recv()
    total = buf[0]
    for j in range(1, size):
        total = total + buf[j]
    return total, every


def all_sum(vec, ty, tx, ybuf, xbuf, ys, yr, xs, xr, beside, later):
    total, sent_y = group_sum(vec, ybuf, ys, yr, ty, NY, lambda j: (j, tx), beside)
    total, sent_x = group_sum(total, xbuf, xs, xr, tx, NX, lambda j: (ty, j), later)
    sent_y.wait_send()
    sent_x.wait_send()
    return total


def remote_to(src, dst, ssem, rsem, dev):
    return pltpu.make_async_remote_copy(
        src_ref=src, dst_ref=dst, send_sem=ssem, recv_sem=rsem, device_id=dev, device_id_type=MESH
    )


def half_sum(total, high):
    lane = lax.broadcasted_iota(jnp.int32, (1, 128), 1)
    return jnp.sum(jnp.where((lane >= 64) == high, total, 0.0), axis=1, keepdims=True)


def step_size(total):
    return RATE * lax.rsqrt(jnp.broadcast_to(half_sum(total, False) / AREA + EPS, (8, 128)))


SUM_SCRATCH = [
    pltpu.VMEM((NY, 1, 128), f32),
    pltpu.VMEM((NX, 1, 128), f32),
    pltpu.SemaphoreType.DMA((1,)),
    pltpu.SemaphoreType.DMA((1,)),
    pltpu.SemaphoreType.DMA((1,)),
    pltpu.SemaphoreType.DMA((1,)),
]


def squares(value):
    return jnp.sum((value * value).reshape(-1, 8, 128), axis=0)


def spread_kernel(g_ref, mis_ref, tot_ref, sum_ref, alpha_ref, zeros_ref, zsend, ysend, zrecv, yrecv, ss, rs, *sums):
    ty, tx, left, right, above, below = places()
    bar = group_barrier(ty, tx)
    odd = lax.rem(tx, 2) == 1
    pieces = ENDS + (MID,)

    def z(p, ct, i):
        src, dst = zsend.at[p, ct, :, :, pieces[i], :], zrecv.at[p, 1 - ct, :, :, pieces[i], :]
        return remote(src, dst, ss, rs, 6 * p + 3 * ct + i, (left, right)[ct])

    def y(p, e, ct):
        return remote(ysend.at[p, e, ct], yrecv.at[p, 1 - e, ct], ss, rs, 12 + 4 * p + 2 * e + ct, (above, below)[e])

    def put_z(p, ct, i, value):
        zsend[p, ct, :, :, pieces[i], :] = value.astype(bf16)
        z(p, ct, i).start()

    def put_y(p, e, ct, value):
        ysend[p, e, ct] = value.astype(bf16)
        y(p, e, ct).start()

    def got_z(p, ct, i):
        z(p, 1 - ct, i).wait_recv()
        return zrecv[p, ct, :, :, pieces[i], :].astype(f32)

    def got_y(p, e, ct):
        y(p, 1 - e, ct).wait_recv()
        return yrecv[p, e, ct].astype(f32)

    def raw(p, ct, i):
        return g_ref[p, :, :, ct, pieces[i], :]

    def keep(p, ct, i, value):
        tot_ref[p, :, :, ct, pieces[i], :] = value
        return value

    def kept(p, ct, i):
        return tot_ref[p, :, :, ct, pieces[i], :]

    pl.semaphore_wait(bar, NY + NX - 2)

    @pl.when(jnp.logical_not(odd))
    def _():
        for e in (1, 0):
            put_y(1, e, 0, raw(1, 0, e))
            for p in (1, 0):
                put_z(p, 1, e, raw(p, 1, e))
        for e in (1, 0):
            put_z(0, 0, e, raw(0, 0, e))
        for p in range(2):
            for ct in range(2):
                put_z(p, ct, 2, raw(p, ct, 2))
        for e in (1, 0):
            put_y(0, e, 0, keep(0, 0, e, raw(0, 0, e) + got_z(0, 0, e)))
        for e in (0, 1):
            put_z(1, 0, e, keep(1, 0, e, raw(1, 0, e) + got_y(1, e, 0)))
        for p in range(2):
            keep(p, 0, 2, raw(p, 0, 2) + got_z(p, 0, 2))
        keep(1, 0, 0, kept(1, 0, 0) + got_z(1, 0, 0))
        keep(0, 0, 0, kept(0, 0, 0) + got_y(0, 0, 0))

    @pl.when(odd)
    def _():
        for e in (1, 0):
            put_y(1, e, 1, raw(1, 1, e))
            put_z(0, 1, e, raw(0, 1, e))
        for p in (1, 0):
            for e in (1, 0):
                put_y(p, e, 0, keep(p, 0, e, raw(p, 0, e) + got_z(p, 0, e)))
        for p in range(2):
            put_z(p, 1, 2, raw(p, 1, 2))
        for e in (1, 0):
            put_y(0, e, 1, keep(0, 1, e, raw(0, 1, e) + got_z(0, 1, e)))
        for e in (0, 1):
            put_z(1, 1, e, keep(1, 1, e, raw(1, 1, e) + got_y(1, e, 1)))
        for p in range(2):
            keep(p, 0, 2, raw(p, 0, 2) + got_z(p, 0, 2))
        for p in (1, 0):
            keep(p, 0, 0, kept(p, 0, 0) + got_y(p, 0, 0))

    sq = squares(tot_ref[:, :, :, 0, 0:256, :])

    def beside():
        @pl.when(jnp.logical_not(odd))
        def _():
            keep(1, 0, 1, kept(1, 0, 1) + got_z(1, 0, 1))
            keep(0, 0, 1, kept(0, 0, 1) + got_y(0, 1, 0))

        @pl.when(odd)
        def _():
            for p in (1, 0):
                put_z(p, 0, 0, kept(p, 0, 0))
                put_z(p, 0, 2, kept(p, 0, 2))
            for p in (1, 0):
                put_z(p, 0, 1, keep(p, 0, 1, kept(p, 0, 1) + got_y(p, 1, 0)))
            for p in range(2):
                keep(p, 1, 2, raw(p, 1, 2) + got_z(p, 1, 2))
            for e in range(2):
                keep(0, 1, e, kept(0, 1, e) + got_y(0, e, 1))
                keep(1, 1, e, kept(1, 1, e) + got_z(1, 1, e))

    def later():
        zeros_ref[...] = jnp.zeros_like(zeros_ref)

        @pl.when(jnp.logical_not(odd))
        def _():
            for i in (0, 2, 1):
                for p in (1, 0):
                    keep(p, 1, i, got_z(p, 1, i))

    total = all_sum(sum_vector(sq, mis_ref[...]), ty, tx, *sums, beside=beside, later=later)
    sum_ref[...] = jnp.broadcast_to(total, (8, 128))
    alpha_ref[...] = step_size(total)
    for p in range(2):
        for e in range(2):
            y(p, e, 0).wait_send()
        for ct in range(2):
            for i in range(3):
                z(p, ct, i).wait_send()

    @pl.when(odd)
    def _():
        for p in range(2):
            for e in range(2):
                y(p, e, 1).wait_send()


def final_kernel(
    g_ref, mis_ref, tot_ref, alpha_ref, before, mixed, sum_ref, zsend, ysend, zrecv, yrecv, own, ss, rs, *sums
):
    ty, tx, left, right, above, below = places()
    bar = group_barrier(ty, tx)
    odd = lax.rem(tx, 2) == 1
    pieces = ENDS + (MID,)

    def z(p, i):
        return remote(zsend.at[p, :, :, pieces[i], :], zrecv.at[p, :, :, pieces[i], :], ss, rs, 3 * p + i, right)

    def y(p, ct):
        return remote(ysend.at[p, ct], yrecv.at[p, ct], ss, rs, 6 + 2 * p + ct, below)

    def put_z(p, i, value):
        zsend[p, :, :, pieces[i], :] = value.astype(bf16)
        z(p, i).start()

    def put_y(p, ct, value):
        ysend[p, ct] = value.astype(bf16)
        y(p, ct).start()

    def got_z(p, i):
        z(p, i).wait_recv()
        return zrecv[p, :, :, pieces[i], :].astype(f32)

    def got_y(p, ct):
        y(p, ct).wait_recv()
        return yrecv[p, ct].astype(f32)

    def raw(p, ct, i):
        return g_ref[p, :, :, ct, pieces[i], :]

    pl.semaphore_wait(bar, NY + NX - 2)

    @pl.when(jnp.logical_not(odd))
    def _():
        put_y(1, 0, raw(1, 0, 1))
        for p, i in ((1, 1), (0, 1), (1, 0), (0, 0), (1, 2), (0, 2)):
            put_z(p, i, raw(p, 1, i))
        put_y(0, 0, raw(0, 0, 1) + got_z(0, 1))

    @pl.when(odd)
    def _():
        put_y(1, 1, raw(1, 1, 1))
        put_z(0, 1, raw(0, 1, 1))
        for p in (1, 0):
            put_y(p, 0, raw(p, 0, 1) + got_z(p, 1))
        put_z(0, 0, raw(0, 1, 0))
        put_z(1, 2, raw(1, 1, 2))
        put_z(0, 2, raw(0, 1, 2))
        put_z(1, 0, raw(1, 1, 0) + got_y(1, 1))

    sq = jnp.zeros((8, 128), f32)
    for p in range(2):
        value = raw(p, 0, 2) + got_z(p, 2)
        own[p, :, :, MID, :] = value
        sq = sq + squares(value)
    for p in (1, 0):
        value = raw(p, 0, 0) + got_y(p, 0) + got_z(p, 0)
        own[p, :, :, ENDS[0], :] = value
        sq = sq + squares(value)
    pos = lax.broadcasted_iota(jnp.int32, (256, 256), 0)
    col = lax.broadcasted_iota(jnp.int32, (256, 256), 1)
    perm = ((pos & 127) * 2 + (pos >> 7) == col).astype(f32).astype(bf16)

    def weave(dst, pln, value):
        for rp in range(2):
            rest = jnp.concatenate([value[rp, 0], value[rp, 1]], axis=1)
            hi = rest.astype(bf16)
            lo = (rest - hi.astype(f32)).astype(bf16)
            w = dot(hi, perm) + dot(lo, perm)
            for h in range(2):
                dst[pln, h, pl.ds(rp, 256, stride=2), :] = w[:, h * 128 : h * 128 + 128]

    def beside():
        for pln in range(2):
            weave(mixed, pln, own[pln])

    def later():
        for pln in range(2):
            weave(before, pln, alpha_ref[0:1, :] * tot_ref[pln, :, :, 0, 0:256, :])

    total = all_sum(sum_vector(sq, mis_ref[...]), ty, tx, *sums, beside=beside, later=later)
    sum_ref[...] = jnp.broadcast_to(total, (8, 128))
    for p in range(2):
        for i in (0, 2):
            z(p, i).wait_send()
        y(p, 0).wait_send()
    z(0, 1).wait_send()

    @pl.when(odd)
    def _():
        y(1, 1).wait_send()

    @pl.when(jnp.logical_not(odd))
    def _():
        z(1, 1).wait_send()


def finish_kernel(spec_ref, before, mixed, sum1_ref, sum2_ref, out_ref, misfit_ref, new, sems):
    alpha = step_size(sum2_ref[0:1, :])[0:1, :]
    copies = []
    for pln in range(2):
        for part in range(2):
            rows = slice(256 * part, 256 * part + 256)
            for h in range(2):
                cols = slice(h * 128, h * 128 + 128)
                new[pln, rows, cols] = spec_ref[pln, rows, cols] - before[pln, h, rows] - alpha * mixed[pln, h, rows]
            copies.append(pltpu.make_async_copy(new.at[pln, rows], out_ref.at[pln, rows], sems.at[2 * pln + part]))
            copies[-1].start()
    misfit_ref[0] = half_sum(sum1_ref[0:1, :], True)[0, 0] / MIS_TOTAL
    misfit_ref[1] = half_sum(sum2_ref[0:1, :], True)[0, 0] / MIS_TOTAL
    for copy in copies:
        copy.wait()


VM = pl.BlockSpec(memory_space=pltpu.VMEM)
SM = pl.BlockSpec(memory_space=pltpu.SMEM)
HBM = pl.BlockSpec(memory_space=pltpu.HBM)
ACC = (2, 2, 2, 2, 512, 128)


def params(mib, cid=None):
    if cid is None:
        return pltpu.CompilerParams(vmem_limit_bytes=mib << 20)
    return pltpu.CompilerParams(vmem_limit_bytes=mib << 20, collective_id=cid, has_side_effects=True)


def shape(dims, t):
    return jax.ShapeDtypeStruct(dims, t)


def patterns(first, n, off, *args):
    off = pltpu.with_memory_space_constraint(off, pltpu.HBM)
    return pl.pallas_call(
        functools.partial(pattern_kernel, first),
        out_shape=(shape(ACC, f32), shape((8, 128), f32)),
        in_specs=[SM, HBM] + [VM] * len(args),
        out_specs=(VM, VM),
        input_output_aliases={2: 0},
        scratch_shapes=[
            pltpu.VMEM(EXT, f32),
            pltpu.VMEM((KEEP, 2, 2, 2, 128, 128), f32),
            pltpu.VMEM((2, 8, 128), f32),
            *[pltpu.VMEM((KEEP, 2, 256, 256), bf16)] * 4,
            pltpu.SMEM((2, 24), jnp.int32),
            pltpu.SemaphoreType.DMA((1,)),
        ],
        compiler_params=params(28),
        name="patterns",
    )(n, off, *args)


def body(specimen, probe_wave, amplitudes, counts, offsets):
    off = offsets[0].T
    ext, probe, tab, amp, zeros = pl.pallas_call(
        halo_kernel,
        out_shape=(
            shape(EXT, bf16),
            shape((2, 2, 2, 128, 128), f32),
            shape((4, 256, 256), bf16),
            shape((24, 256, 256), bf16),
            shape(ACC, f32),
        ),
        in_specs=[HBM] * 4,
        out_specs=(VM,) * 5,
        scratch_shapes=[
            pltpu.VMEM((2, 512, 256), f32),
            pltpu.VMEM((2, 256, 256), f32),
            pltpu.VMEM((4, 256, 256), f32),
            pltpu.VMEM((2, 2, 512, 128), f32),
            pltpu.SemaphoreType.DMA((5,)),
            pltpu.SemaphoreType.DMA((8,)),
            pltpu.SemaphoreType.DMA((8,)),
        ],
        compiler_params=params(16, 0),
        name="halo",
    )(*[pltpu.with_memory_space_constraint(x, pltpu.HBM) for x in (specimen, probe_wave, jnp.asarray(tables()), amplitudes[0])])
    g1, mis1 = patterns(True, counts, off, zeros, ext, probe, tab, amp)
    tot1, sum1, alpha1, zeros = pl.pallas_call(
        spread_kernel,
        out_shape=(shape(EXT, f32), shape((8, 128), f32), shape((8, 128), f32), shape(ACC, f32)),
        in_specs=[VM] * 2,
        out_specs=(VM,) * 4,
        scratch_shapes=[
            pltpu.VMEM((2, 2, 2, 2, 384, 128), bf16),
            pltpu.VMEM((2, 2, 2, 2, 2, 128, 128), bf16),
            pltpu.VMEM((2, 2, 2, 2, 384, 128), bf16),
            pltpu.VMEM((2, 2, 2, 2, 2, 128, 128), bf16),
            pltpu.SemaphoreType.DMA((20,)),
            pltpu.SemaphoreType.DMA((20,)),
            *SUM_SCRATCH,
        ],
        compiler_params=params(16, 1),
        name="spread",
    )(g1, mis1)
    g2, mis2 = patterns(False, counts, off, zeros, ext, tot1, alpha1, probe, tab, amp)
    before, mixed, sum2 = pl.pallas_call(
        final_kernel,
        out_shape=(shape((2, 2, 512, 128), f32), shape((2, 2, 512, 128), f32), shape((8, 128), f32)),
        in_specs=[VM] * 4,
        out_specs=(VM,) * 3,
        scratch_shapes=[
            pltpu.VMEM((2, 2, 2, 384, 128), bf16),
            pltpu.VMEM((2, 2, 2, 2, 128, 128), bf16),
            pltpu.VMEM((2, 2, 2, 384, 128), bf16),
            pltpu.VMEM((2, 2, 2, 2, 128, 128), bf16),
            pltpu.VMEM((2, 2, 2, 256, 128), f32),
            pltpu.SemaphoreType.DMA((10,)),
            pltpu.SemaphoreType.DMA((10,)),
            *SUM_SCRATCH,
        ],
        compiler_params=params(16, 2),
        name="final",
    )(g2, mis2, tot1, alpha1)
    return pl.pallas_call(
        finish_kernel,
        out_shape=(shape((2, 512, 256), f32), shape((2,), f32)),
        in_specs=[VM] * 5,
        out_specs=(pl.BlockSpec(memory_space=pl.ANY), SM),
        scratch_shapes=[pltpu.VMEM((2, 512, 256), f32), pltpu.SemaphoreType.DMA((4,))],
        compiler_params=params(16),
        name="finish",
    )(specimen, before, mixed, sum1, sum2)


def solution(mesh):
    return jax.shard_map(
        body,
        mesh=mesh,
        in_specs=(P(None, "ty", "tx"), P(), P(("ty", "tx"), None, None, None), P(("ty", "tx")), P(("ty", "tx"), None, None)),
        out_specs=(P(None, "ty", "tx"), P()),
        check_vma=False,
    )
```

```python
import functools

import jax
import jax.numpy as jnp
import ml_dtypes
import numpy as np
from jax import lax
from jax.experimental import pallas as pl
from jax.experimental.pallas import tpu as pltpu
from jax.sharding import PartitionSpec as P

MESH = pl.DeviceIdType.MESH
f32, bf16 = jnp.float32, jnp.bfloat16
NY, NX = 16, 8
ENDS = (slice(0, 128), slice(256, 384))
MID = slice(128, 256)
U = 6
KEEP = 6
ROWS = 32
EXT = (2, 2, 2, 2, 384, 128)
AREA = 8192.0 * 2048.0
RATE = 0.1
EPS = 1e-6
FLOOR_INV = 2.0
MIS_TOTAL = 1024.0 * 65536.0


def tables():
    n = 256
    k = np.arange(n)
    ang = (k[:, None] * k[None, :] % n) * (2 * np.pi / n)
    fr, fi = np.cos(ang) / 16.0, -np.sin(ang) / 16.0
    out = []
    for p in range(2):
        r, i = fr[:128, p::2], fi[:128, p::2]
        out.append(np.block([[r, -i], [i, r]]))
    for p in range(2):
        out.append(out[p].T)
    return np.stack(out).astype(ml_dtypes.bfloat16).astype(np.float32)


def dot(a, b):
    return jnp.dot(a, b, preferred_element_type=f32)


def remote(src, dst, sems, rems, i, dev):
    return pltpu.make_async_remote_copy(
        src_ref=src, dst_ref=dst, send_sem=sems.at[i], recv_sem=rems.at[i], device_id=dev, device_id_type=MESH
    )


def places():
    ty, tx = lax.axis_index("ty"), lax.axis_index("tx")
    left, right = (ty, lax.rem(tx + NX - 1, NX)), (ty, lax.rem(tx + 1, NX))
    above, below = (lax.rem(ty + NY - 1, NY), tx), (lax.rem(ty + 1, NY), tx)
    return ty, tx, left, right, above, below


def halo_kernel(
    spec_hbm, probe_hbm, tab_hbm, amp_hbm, split_ref, tab_out, amp_out, zeros_ref, wide_ref, ext_ref, spec_ref, probe_ref, tab_ref, tmp, ls, ss, rs
):
    ty, tx, left, right, above, below = places()
    bar = pltpu.get_barrier_semaphore()
    for dev in (right, below):
        pl.semaphore_signal(bar, inc=1, device_id=dev, device_id_type=MESH)
    upper, lower = (slice(None), slice(0, 256)), (slice(None), slice(256, 512))
    pairs = ((spec_hbm.at[upper], spec_ref.at[upper]), (spec_hbm.at[lower], spec_ref.at[lower]), (probe_hbm, probe_ref), (tab_hbm, tab_ref), (amp_hbm, amp_out))
    loads = [pltpu.make_async_copy(src, dst, ls.at[i]) for i, (src, dst) in enumerate(pairs)]
    for load in loads:
        load.start()
    pos = lax.broadcasted_iota(jnp.int32, (256, 256), 0)
    col = lax.broadcasted_iota(jnp.int32, (256, 256), 1)
    perm = ((col & 127) * 2 + (col >> 7) == pos).astype(f32).astype(bf16)

    def split(rows, pln):
        n = rows.stop - rows.start
        w = dot(spec_ref[pln, rows].astype(bf16), perm)
        tmp[pln, 0, rows] = w[:, :128]
        tmp[pln, 1, rows] = w[:, 128:]
        half = slice(rows.start // 2, rows.stop // 2)
        for rp in range(2):
            for cp in range(2):
                part = tmp[pln, cp, pl.ds(rows.start + rp, n // 2, stride=2), :]
                ext_ref[pln, rp, cp, 0, half, :] = part.astype(bf16)

    loads[0].wait()
    split(slice(0, 256), 0)
    pl.semaphore_wait(bar, 2)
    top, low = ENDS

    def block(pln, ct, rows):
        return ext_ref.at[pln, :, :, ct, rows, :]

    a = remote(block(0, 0, top), block(0, 0, low), ss, rs, 0, above)
    c = remote(block(1, 0, top), block(1, 1, top), ss, rs, 1, left)
    b = remote(block(1, 0, top), block(1, 0, low), ss, rs, 2, above)
    d = remote(block(0, 0, top), block(0, 1, top), ss, rs, 3, left)
    e = [remote(block(p, 0, MID), block(p, 1, MID), ss, rs, (7, 4)[p], left) for p in range(2)]
    corner0 = remote(block(0, 0, low), block(0, 1, low), ss, rs, 5, left)
    corner1_up = remote(block(1, 1, top), block(1, 1, low), ss, rs, 6, above)
    corner1_left = remote(block(1, 0, low), block(1, 1, low), ss, rs, 6, left)
    odd = lax.rem(tx, 2) == 1
    a.start()
    split(slice(0, 256), 1)
    for copy in (c, b, d):
        copy.start()
    loads[1].wait()
    for pln in range(2):
        split(slice(256, 512), pln)
    for copy in e:
        copy.start()
    loads[2].wait()
    loads[3].wait()
    tab_out[...] = tab_ref[...].astype(bf16)
    for pln in range(2):
        value = probe_ref[pln]
        terms = 0.0
        for _ in range(3):
            part = value.astype(bf16)
            value = value - part.astype(f32)
            terms = terms + dot(part, perm)
        tmp[pln, 0, 0:256] = terms[:, :128]
        tmp[pln, 1, 0:256] = terms[:, 128:]
    for pln in range(2):
        for q in range(2):
            for cp in range(2):
                split_ref[pln, q, cp] = tmp[pln, cp, pl.ds(q, 128, stride=2), :]
    zeros_ref[...] = jnp.zeros_like(zeros_ref)

    def widen(pln, ct, rows):
        wide_ref[pln, :, :, ct, rows, :] = ext_ref[pln, :, :, ct, rows, :].astype(f32)

    for pln in range(2):
        widen(pln, 0, slice(0, 256))
    c.wait_recv()

    @pl.when(odd)
    def _():
        corner1_up.start()

    a.wait_recv()
    corner0.start()
    b.wait_recv()

    @pl.when(odd)
    def _():
        corner1_left.start()

    d.wait_recv()
    for copy in e:
        copy.wait_recv()
    for pln in range(2):
        widen(pln, 1, slice(0, 256))
        widen(pln, 0, low)
    corner0.wait_recv()
    corner1_up.wait_recv()
    for pln in range(2):
        widen(pln, 1, low)
    loads[4].wait()
    for copy in (a, c, b, d, *e, corner0):
        copy.wait_send()

    @pl.when(odd)
    def _():
        corner1_up.wait_send()
        corner1_left.wait_send()


def pattern_kernel(first, n_ref, off_hbm, zeros_ref, ext_ref, *refs):
    *refs, off_ref, sems = refs
    load = pltpu.make_async_copy(off_hbm, off_ref, sems.at[0])
    load.start()
    if first:
        probe_ref, tab_ref, amp_ref, acc, mis_ref, _, prol, macc, W, L, R, Y = refs
        obj = ext_ref
    else:
        tot_ref, alpha_ref, probe_ref, tab_ref, amp_ref, acc, mis_ref, obj, prol, macc, W, L, R, Y = refs
        obj[...] = ext_ref[...] - alpha_ref[0:1, :] * tot_ref[...]
    macc[0] = jnp.zeros((8, 128), f32)
    lane = lax.broadcasted_iota(jnp.int32, (128, 128), 1)
    load.wait()
    n = n_ref[0]
    halves = (slice(0, 128), slice(128, 256))

    def geometry(i):
        live = i < n
        s = jnp.minimum(i, n - 1)
        r = off_ref[0, s] & 511
        c = off_ref[1, s] & 255
        rho = r & 1
        start = (r >> 1, (r + rho) >> 1)
        masks = [lane * 2 + cp >= c for cp in range(2)]
        return live, s, c, start, (rho, 1 - rho), masks

    def make_wave(k, i):
        _, s, c, start, par, masks = geometry(i)
        for cp in range(2):
            pp = cp ^ (c & 1)
            shift = ((c + pp - cp) >> 1) & 127
            for q in range(2):
                sl = pl.ds(start[q], 128)
                p = [pltpu.roll(probe_ref[pln, q, pp], shift, 1) for pln in range(2)]
                o = [
                    jnp.where(masks[cp], obj[pln, par[q], cp, 0, sl, :], obj[pln, par[q], cp, 1, sl, :])
                    for pln in range(2)
                ]
                for pln in range(2):
                    prol[k, pln, q, cp] = p[pln]
                W[k, q, 0:128, halves[cp]] = (p[0] * o[0] - p[1] * o[1]).astype(bf16)
                W[k, q, 128:256, halves[cp]] = (p[0] * o[1] + p[1] * o[0]).astype(bf16)

    def products(accs):
        state = dict(staged=0, half=0, waiting=None)
        count = 256 // ROWS

        def take():
            if state["waiting"] is not None:
                state["waiting"]()
            state["waiting"] = None

        def start(weights, lhs, use):
            staged, base = state["staged"], state["half"] * count
            state["staged"], state["half"] = 1 - staged, 1 - state["half"]
            for unit in range(2):
                pltpu.matmul_push_rhs(weights[unit], staged, unit)
            for j in range(count):
                for unit in range(2):
                    pltpu.matmul_acc_lhs(accs[unit][base + j], lhs(unit, j), staged if j == 0 else None)
            take()

            def results():
                for j in range(count):
                    use(j, pltpu.matmul_pop(accs[0][base + j]), pltpu.matmul_pop(accs[1][base + j]))

            state["waiting"] = results

        return start, take

    def run(*accs):
        half = len(accs) // 2
        start, take = products((accs[:half], accs[half:]))

        def rows_forward(k, i):
            def use(j, t0, t1):
                pln, u = j * ROWS // 128, j * ROWS % 128
                for h, near in enumerate(((t0 + t1).astype(bf16), (t0 - t1).astype(bf16))):
                    for cp in range(2):
                        L[k, cp, 128 * h + u : 128 * h + u + ROWS, halves[pln]] = near[:, halves[cp]]

            start([W[k, 0], W[k, 1]], lambda unit, j: tab_ref[unit, j * ROWS : (j + 1) * ROWS], use)

        def columns_forward(k, i):
            live, s, *_ = geometry(i)
            mis = [jnp.zeros((8, 128), f32)]

            def use(j, x0, x1):
                rows = slice(j * ROWS, (j + 1) * ROWS)
                res = []
                for h in range(2):
                    spectrum = x0 + x1 if h == 0 else x0 - x1
                    sr, si = spectrum[:, :128], spectrum[:, 128:]
                    a = amp_ref[s, rows, halves[h]].astype(f32)
                    m2 = jnp.maximum(sr * sr + si * si, 1e-30)
                    inv = lax.rsqrt(m2)
                    dm = m2 * inv - a
                    mis[0] = mis[0] + jnp.sum((dm * dm).reshape(ROWS // 8, 8, 128), axis=0)
                    f = 1.0 - a * jnp.minimum(inv, FLOOR_INV)
                    res.append((sr * f, si * f))
                for pln in range(2):
                    R[k, 0, rows, halves[pln]] = (res[0][pln] + res[1][pln]).astype(bf16)
                    R[k, 1, rows, halves[pln]] = (res[0][pln] - res[1][pln]).astype(bf16)
                if j == 256 // ROWS - 1:
                    macc[jnp.where(live, 0, 1)] += mis[0]

            start([tab_ref[2], tab_ref[3]], lambda unit, j: L[k, unit, j * ROWS : (j + 1) * ROWS], use)

        def two_rows(ref, j):
            h = ROWS // 2
            return jnp.concatenate([ref[j * h : (j + 1) * h], ref[128 + j * h : 128 + (j + 1) * h]], axis=0)

        def columns_back(k, i):
            h = ROWS // 2

            def use(j, *terms):
                for cp, t in enumerate(terms):
                    for q in range(2):
                        y = (t[:h] + t[h:] if q == 0 else t[:h] - t[h:]).astype(bf16)
                        Y[k, q, j * h : (j + 1) * h, halves[cp]] = y[:, :128]
                        Y[k, q, 128 + j * h : 128 + (j + 1) * h, halves[cp]] = y[:, 128:]

            start([tab_ref[0], tab_ref[1]], lambda unit, j: two_rows(R.at[k, unit], j), use)

        def rows_back(k, i):
            live, s, c, first_row, par, masks = geometry(i)
            h = ROWS // 2

            def use(j, *terms):
                for q, t in enumerate(terms):
                    sl = pl.ds(jnp.where(live, first_row[q], 384) + j * h, h)
                    rows = slice(j * h, (j + 1) * h)
                    for cp in range(2):
                        pr, pi = prol[k, 0, q, cp, rows], prol[k, 1, q, cp, rows]
                        zr, zi = t[:h, halves[cp]], t[h:, halves[cp]]
                        grad = (pr * zr + pi * zi, pr * zi - pi * zr)
                        mask = masks[cp][:h]
                        for pln in range(2):
                            own = acc.at[pln, par[q], cp, 0, sl, :]
                            right = acc.at[pln, par[q], cp, 1, sl, :]
                            pltpu.store(own, own[...] + grad[pln], mask=mask)
                            pltpu.store(right, right[...] + grad[pln], mask=jnp.logical_not(mask))

            start([Y[k, 0], Y[k, 1]], lambda unit, j: two_rows(tab_ref.at[2 + unit], j), use)

        stages = (make_wave, rows_forward, columns_forward, columns_back, rows_back)

        def group(j, _):
            for t in range(U + len(stages) - 1):
                for late, stage in enumerate(stages):
                    if 0 <= t - late < U:
                        stage((t - late) % KEEP, j * U + t - late)
            take()
            return 0

        lax.fori_loop(0, (n + U - 1) // U, group, 0)

    accumulators = 2 * 256 // ROWS
    pl.run_scoped(
        run,
        *[pltpu.ACC(mxu_id=0)((ROWS, 256), f32)] * accumulators,
        *[pltpu.ACC(mxu_id=1)((ROWS, 256), f32)] * accumulators,
    )
    mis_ref[...] = macc[0]


def group_barrier(ty, tx):
    bar = pltpu.get_barrier_semaphore()
    for k in [1, NY - 1] + list(range(2, NY - 1)):
        pl.semaphore_signal(bar, inc=1, device_id=(lax.rem(ty + k, NY), tx), device_id_type=MESH)
        if k in (1, NY - 1):
            x = 1 if k == 1 else NX - 1
            pl.semaphore_signal(bar, inc=1, device_id=(ty, lax.rem(tx + x, NX)), device_id_type=MESH)
    for k in range(2, NX - 1):
        pl.semaphore_signal(bar, inc=1, device_id=(ty, lax.rem(tx + k, NX)), device_id_type=MESH)
    return bar


def sum_vector(sq, mis):
    lane = lax.broadcasted_iota(jnp.int32, (1, 128), 1)
    sq = jnp.sum(sq, axis=0, keepdims=True)
    mis = jnp.sum(mis, axis=0, keepdims=True)
    return jnp.where(lane < 64, sq + pltpu.roll(sq, 64, 1), mis + pltpu.roll(mis, 64, 1))


def group_sum(vec, buf, ss, rs, me, size, device, beside):
    buf[me] = vec
    for k in range(1, size):
        remote_to(buf.at[me], buf.at[me], ss.at[0], rs.at[0], device(lax.rem(me + k, size))).start()
    beside()
    rest = buf.at[pl.ds(0, size - 1)]
    every = remote_to(rest, rest, ss.at[0], rs.at[0], device(lax.rem(me + 1, size)))
    every.wait_recv()
    total = buf[0]
    for j in range(1, size):
        total = total + buf[j]
    return total, every


def all_sum(vec, ty, tx, ybuf, xbuf, ys, yr, xs, xr, beside, later):
    total, sent_y = group_sum(vec, ybuf, ys, yr, ty, NY, lambda j: (j, tx), beside)
    total, sent_x = group_sum(total, xbuf, xs, xr, tx, NX, lambda j: (ty, j), later)
    sent_y.wait_send()
    sent_x.wait_send()
    return total


def remote_to(src, dst, ssem, rsem, dev):
    return pltpu.make_async_remote_copy(
        src_ref=src, dst_ref=dst, send_sem=ssem, recv_sem=rsem, device_id=dev, device_id_type=MESH
    )


def half_sum(total, high):
    lane = lax.broadcasted_iota(jnp.int32, (1, 128), 1)
    return jnp.sum(jnp.where((lane >= 64) == high, total, 0.0), axis=1, keepdims=True)


def step_size(total):
    return RATE * lax.rsqrt(jnp.broadcast_to(half_sum(total, False) / AREA + EPS, (8, 128)))


SUM_SCRATCH = [
    pltpu.VMEM((NY, 1, 128), f32),
    pltpu.VMEM((NX, 1, 128), f32),
    pltpu.SemaphoreType.DMA((1,)),
    pltpu.SemaphoreType.DMA((1,)),
    pltpu.SemaphoreType.DMA((1,)),
    pltpu.SemaphoreType.DMA((1,)),
]


def squares(value):
    return jnp.sum((value * value).reshape(-1, 8, 128), axis=0)


def spread_kernel(g_ref, mis_ref, tot_ref, sum_ref, alpha_ref, zeros_ref, zsend, ysend, zrecv, yrecv, ss, rs, *sums):
    ty, tx, left, right, above, below = places()
    bar = group_barrier(ty, tx)
    odd = lax.rem(tx, 2) == 1
    pieces = ENDS + (MID,)

    def z(p, ct, i):
        src, dst = zsend.at[p, ct, :, :, pieces[i], :], zrecv.at[p, 1 - ct, :, :, pieces[i], :]
        return remote(src, dst, ss, rs, 6 * p + 3 * ct + i, (left, right)[ct])

    def y(p, e, ct):
        return remote(ysend.at[p, e, ct], yrecv.at[p, 1 - e, ct], ss, rs, 12 + 4 * p + 2 * e + ct, (above, below)[e])

    def put_z(p, ct, i, value):
        zsend[p, ct, :, :, pieces[i], :] = value.astype(bf16)
        z(p, ct, i).start()

    def put_y(p, e, ct, value):
        ysend[p, e, ct] = value.astype(bf16)
        y(p, e, ct).start()

    def got_z(p, ct, i):
        z(p, 1 - ct, i).wait_recv()
        return zrecv[p, ct, :, :, pieces[i], :].astype(f32)

    def got_y(p, e, ct):
        y(p, 1 - e, ct).wait_recv()
        return yrecv[p, e, ct].astype(f32)

    def raw(p, ct, i):
        return g_ref[p, :, :, ct, pieces[i], :]

    def keep(p, ct, i, value):
        tot_ref[p, :, :, ct, pieces[i], :] = value
        return value

    def kept(p, ct, i):
        return tot_ref[p, :, :, ct, pieces[i], :]

    pl.semaphore_wait(bar, NY + NX - 2)

    @pl.when(jnp.logical_not(odd))
    def _():
        for e in (1, 0):
            put_y(1, e, 0, raw(1, 0, e))
            for p in (1, 0):
                put_z(p, 1, e, raw(p, 1, e))
        for e in (1, 0):
            put_z(0, 0, e, raw(0, 0, e))
        for p in range(2):
            for ct in range(2):
                put_z(p, ct, 2, raw(p, ct, 2))
        for e in (1, 0):
            put_y(0, e, 0, keep(0, 0, e, raw(0, 0, e) + got_z(0, 0, e)))
        for e in (0, 1):
            put_z(1, 0, e, keep(1, 0, e, raw(1, 0, e) + got_y(1, e, 0)))
        for p in range(2):
            keep(p, 0, 2, raw(p, 0, 2) + got_z(p, 0, 2))
        keep(1, 0, 0, kept(1, 0, 0) + got_z(1, 0, 0))
        keep(0, 0, 0, kept(0, 0, 0) + got_y(0, 0, 0))

    @pl.when(odd)
    def _():
        for e in (1, 0):
            put_y(1, e, 1, raw(1, 1, e))
            put_z(0, 1, e, raw(0, 1, e))
        for p in (1, 0):
            for e in (1, 0):
                put_y(p, e, 0, keep(p, 0, e, raw(p, 0, e) + got_z(p, 0, e)))
        for p in range(2):
            put_z(p, 1, 2, raw(p, 1, 2))
        for e in (1, 0):
            put_y(0, e, 1, keep(0, 1, e, raw(0, 1, e) + got_z(0, 1, e)))
        for e in (0, 1):
            put_z(1, 1, e, keep(1, 1, e, raw(1, 1, e) + got_y(1, e, 1)))
        for p in range(2):
            keep(p, 0, 2, raw(p, 0, 2) + got_z(p, 0, 2))
        for p in (1, 0):
            keep(p, 0, 0, kept(p, 0, 0) + got_y(p, 0, 0))

    sq = squares(tot_ref[:, :, :, 0, 0:256, :])

    def beside():
        @pl.when(jnp.logical_not(odd))
        def _():
            keep(1, 0, 1, kept(1, 0, 1) + got_z(1, 0, 1))
            keep(0, 0, 1, kept(0, 0, 1) + got_y(0, 1, 0))

        @pl.when(odd)
        def _():
            for p in (1, 0):
                put_z(p, 0, 0, kept(p, 0, 0))
                put_z(p, 0, 2, kept(p, 0, 2))
            for p in (1, 0):
                put_z(p, 0, 1, keep(p, 0, 1, kept(p, 0, 1) + got_y(p, 1, 0)))
            for p in range(2):
                keep(p, 1, 2, raw(p, 1, 2) + got_z(p, 1, 2))
            for e in range(2):
                keep(0, 1, e, kept(0, 1, e) + got_y(0, e, 1))
                keep(1, 1, e, kept(1, 1, e) + got_z(1, 1, e))

    def later():
        zeros_ref[...] = jnp.zeros_like(zeros_ref)

        @pl.when(jnp.logical_not(odd))
        def _():
            for i in (0, 2, 1):
                for p in (1, 0):
                    keep(p, 1, i, got_z(p, 1, i))

    total = all_sum(sum_vector(sq, mis_ref[...]), ty, tx, *sums, beside=beside, later=later)
    sum_ref[...] = jnp.broadcast_to(total, (8, 128))
    alpha_ref[...] = step_size(total)
    for p in range(2):
        for e in range(2):
            y(p, e, 0).wait_send()
        for ct in range(2):
            for i in range(3):
                z(p, ct, i).wait_send()

    @pl.when(odd)
    def _():
        for p in range(2):
            for e in range(2):
                y(p, e, 1).wait_send()


def final_kernel(
    g_ref, mis_ref, tot_ref, alpha_ref, before, mixed, sum_ref, zsend, ysend, zrecv, yrecv, own, ss, rs, *sums
):
    ty, tx, left, right, above, below = places()
    bar = group_barrier(ty, tx)
    odd = lax.rem(tx, 2) == 1
    pieces = ENDS + (MID,)

    def z(p, i):
        return remote(zsend.at[p, :, :, pieces[i], :], zrecv.at[p, :, :, pieces[i], :], ss, rs, 3 * p + i, right)

    def y(p, ct):
        return remote(ysend.at[p, ct], yrecv.at[p, ct], ss, rs, 6 + 2 * p + ct, below)

    def put_z(p, i, value):
        zsend[p, :, :, pieces[i], :] = value.astype(bf16)
        z(p, i).start()

    def put_y(p, ct, value):
        ysend[p, ct] = value.astype(bf16)
        y(p, ct).start()

    def got_z(p, i):
        z(p, i).wait_recv()
        return zrecv[p, :, :, pieces[i], :].astype(f32)

    def got_y(p, ct):
        y(p, ct).wait_recv()
        return yrecv[p, ct].astype(f32)

    def raw(p, ct, i):
        return g_ref[p, :, :, ct, pieces[i], :]

    pl.semaphore_wait(bar, NY + NX - 2)

    @pl.when(jnp.logical_not(odd))
    def _():
        put_y(1, 0, raw(1, 0, 1))
        for p, i in ((1, 1), (0, 1), (1, 0), (0, 0), (1, 2), (0, 2)):
            put_z(p, i, raw(p, 1, i))
        put_y(0, 0, raw(0, 0, 1) + got_z(0, 1))

    @pl.when(odd)
    def _():
        put_y(1, 1, raw(1, 1, 1))
        put_z(0, 1, raw(0, 1, 1))
        for p in (1, 0):
            put_y(p, 0, raw(p, 0, 1) + got_z(p, 1))
        put_z(0, 0, raw(0, 1, 0))
        put_z(1, 2, raw(1, 1, 2))
        put_z(0, 2, raw(0, 1, 2))
        put_z(1, 0, raw(1, 1, 0) + got_y(1, 1))

    sq = jnp.zeros((8, 128), f32)
    for p in range(2):
        value = raw(p, 0, 2) + got_z(p, 2)
        own[p, :, :, MID, :] = value
        sq = sq + squares(value)
    for p in (1, 0):
        value = raw(p, 0, 0) + got_y(p, 0) + got_z(p, 0)
        own[p, :, :, ENDS[0], :] = value
        sq = sq + squares(value)
    pos = lax.broadcasted_iota(jnp.int32, (256, 256), 0)
    col = lax.broadcasted_iota(jnp.int32, (256, 256), 1)
    perm = ((pos & 127) * 2 + (pos >> 7) == col).astype(f32).astype(bf16)

    def weave(dst, pln, value):
        for rp in range(2):
            rest = jnp.concatenate([value[rp, 0], value[rp, 1]], axis=1)
            hi = rest.astype(bf16)
            lo = (rest - hi.astype(f32)).astype(bf16)
            w = dot(hi, perm) + dot(lo, perm)
            for h in range(2):
                dst[pln, h, pl.ds(rp, 256, stride=2), :] = w[:, h * 128 : h * 128 + 128]

    def beside():
        for pln in range(2):
            weave(mixed, pln, own[pln])

    def later():
        for pln in range(2):
            weave(before, pln, alpha_ref[0:1, :] * tot_ref[pln, :, :, 0, 0:256, :])

    total = all_sum(sum_vector(sq, mis_ref[...]), ty, tx, *sums, beside=beside, later=later)
    sum_ref[...] = jnp.broadcast_to(total, (8, 128))
    for p in range(2):
        for i in (0, 2):
            z(p, i).wait_send()
        y(p, 0).wait_send()
    z(0, 1).wait_send()

    @pl.when(odd)
    def _():
        y(1, 1).wait_send()

    @pl.when(jnp.logical_not(odd))
    def _():
        z(1, 1).wait_send()


def finish_kernel(spec_ref, before, mixed, sum1_ref, sum2_ref, out_ref, misfit_ref, new, sems):
    alpha = step_size(sum2_ref[0:1, :])[0:1, :]
    copies = []
    for pln in range(2):
        for part in range(2):
            rows = slice(256 * part, 256 * part + 256)
            for h in range(2):
                cols = slice(h * 128, h * 128 + 128)
                new[pln, rows, cols] = spec_ref[pln, rows, cols] - before[pln, h, rows] - alpha * mixed[pln, h, rows]
            copies.append(pltpu.make_async_copy(new.at[pln, rows], out_ref.at[pln, rows], sems.at[2 * pln + part]))
            copies[-1].start()
    misfit_ref[0] = half_sum(sum1_ref[0:1, :], True)[0, 0] / MIS_TOTAL
    misfit_ref[1] = half_sum(sum2_ref[0:1, :], True)[0, 0] / MIS_TOTAL
    for copy in copies:
        copy.wait()


VM = pl.BlockSpec(memory_space=pltpu.VMEM)
SM = pl.BlockSpec(memory_space=pltpu.SMEM)
HBM = pl.BlockSpec(memory_space=pltpu.HBM)
ACC = (2, 2, 2, 2, 512, 128)


def params(mib, cid=None):
    if cid is None:
        return pltpu.CompilerParams(vmem_limit_bytes=mib << 20)
    return pltpu.CompilerParams(vmem_limit_bytes=mib << 20, collective_id=cid, has_side_effects=True)


def shape(dims, t):
    return jax.ShapeDtypeStruct(dims, t)


def patterns(first, n, off, *args):
    off = pltpu.with_memory_space_constraint(off, pltpu.HBM)
    return pl.pallas_call(
        functools.partial(pattern_kernel, first),
        out_shape=(shape(ACC, f32), shape((8, 128), f32)),
        in_specs=[SM, HBM] + [VM] * len(args),
        out_specs=(VM, VM),
        input_output_aliases={2: 0},
        scratch_shapes=[
            pltpu.VMEM(EXT, f32),
            pltpu.VMEM((KEEP, 2, 2, 2, 128, 128), f32),
            pltpu.VMEM((2, 8, 128), f32),
            *[pltpu.VMEM((KEEP, 2, 256, 256), bf16)] * 4,
            pltpu.SMEM((2, 24), jnp.int32),
            pltpu.SemaphoreType.DMA((1,)),
        ],
        compiler_params=params(28),
        name="patterns",
    )(n, off, *args)


def body(specimen, probe_wave, amplitudes, counts, offsets):
    off = offsets[0].T
    probe, tab, amp, zeros, wide = pl.pallas_call(
        halo_kernel,
        out_shape=(
            shape((2, 2, 2, 128, 128), f32),
            shape((4, 256, 256), bf16),
            shape((24, 256, 256), bf16),
            shape(ACC, f32),
            shape(EXT, f32),
        ),
        in_specs=[HBM] * 4,
        out_specs=(VM,) * 5,
        scratch_shapes=[
            pltpu.VMEM(EXT, bf16),
            pltpu.VMEM((2, 512, 256), f32),
            pltpu.VMEM((2, 256, 256), f32),
            pltpu.VMEM((4, 256, 256), f32),
            pltpu.VMEM((2, 2, 512, 128), f32),
            pltpu.SemaphoreType.DMA((5,)),
            pltpu.SemaphoreType.DMA((8,)),
            pltpu.SemaphoreType.DMA((8,)),
        ],
        compiler_params=params(16, 0),
        name="halo",
    )(*[pltpu.with_memory_space_constraint(x, pltpu.HBM) for x in (specimen, probe_wave, jnp.asarray(tables()), amplitudes[0])])
    g1, mis1 = patterns(True, counts, off, zeros, wide, probe, tab, amp)
    tot1, sum1, alpha1, zeros = pl.pallas_call(
        spread_kernel,
        out_shape=(shape(EXT, f32), shape((8, 128), f32), shape((8, 128), f32), shape(ACC, f32)),
        in_specs=[VM] * 2,
        out_specs=(VM,) * 4,
        scratch_shapes=[
            pltpu.VMEM((2, 2, 2, 2, 384, 128), bf16),
            pltpu.VMEM((2, 2, 2, 2, 2, 128, 128), bf16),
            pltpu.VMEM((2, 2, 2, 2, 384, 128), bf16),
            pltpu.VMEM((2, 2, 2, 2, 2, 128, 128), bf16),
            pltpu.SemaphoreType.DMA((20,)),
            pltpu.SemaphoreType.DMA((20,)),
            *SUM_SCRATCH,
        ],
        compiler_params=params(16, 1),
        name="spread",
    )(g1, mis1)
    g2, mis2 = patterns(False, counts, off, zeros, wide, tot1, alpha1, probe, tab, amp)
    before, mixed, sum2 = pl.pallas_call(
        final_kernel,
        out_shape=(shape((2, 2, 512, 128), f32), shape((2, 2, 512, 128), f32), shape((8, 128), f32)),
        in_specs=[VM] * 4,
        out_specs=(VM,) * 3,
        scratch_shapes=[
            pltpu.VMEM((2, 2, 2, 384, 128), bf16),
            pltpu.VMEM((2, 2, 2, 2, 128, 128), bf16),
            pltpu.VMEM((2, 2, 2, 384, 128), bf16),
            pltpu.VMEM((2, 2, 2, 2, 128, 128), bf16),
            pltpu.VMEM((2, 2, 2, 256, 128), f32),
            pltpu.SemaphoreType.DMA((10,)),
            pltpu.SemaphoreType.DMA((10,)),
            *SUM_SCRATCH,
        ],
        compiler_params=params(16, 2),
        name="final",
    )(g2, mis2, tot1, alpha1)
    return pl.pallas_call(
        finish_kernel,
        out_shape=(shape((2, 512, 256), f32), shape((2,), f32)),
        in_specs=[VM] * 5,
        out_specs=(pl.BlockSpec(memory_space=pl.ANY), SM),
        scratch_shapes=[pltpu.VMEM((2, 512, 256), f32), pltpu.SemaphoreType.DMA((4,))],
        compiler_params=params(16),
        name="finish",
    )(specimen, before, mixed, sum1, sum2)


def solution(mesh):
    return jax.shard_map(
        body,
        mesh=mesh,
        in_specs=(P(None, "ty", "tx"), P(), P(("ty", "tx"), None, None, None), P(("ty", "tx")), P(("ty", "tx"), None, None)),
        out_specs=(P(None, "ty", "tx"), P()),
        check_vma=False,
    )
```
